256 devices in a mesh: row: 8 (over z_hi, core), col: 32 (over x, z_lo, y).
Axes of the slice: x: 4, y: 4, z: 8 (z_hi: 4, z_lo: 2; z = z_hi * 2 + z_lo), core: 2. Of those that a mesh axis runs over, the one named last changes fastest.
Arguments:
- tokens: bfloat16 [2048, 12288], P('col', 'row'), may hold values from -12 to 12
- ln_gain: float32 [12288], P('row'), may hold values from 0.25 to 1.75
- ln_bias: float32 [12288], P('row'), may hold values from -3 to 3
- w_qkv: bfloat16 [3, 12288, 12288], P(None, 'row', 'col'), may hold values from -0.078125 to 0.078125
- bias_qkv: float32 [3, 12288], P(None, 'col'), may hold values from -9 to 9
- mask_qkv: int32 [3, 96, 96], P(None, 'row', 'col'), may hold values from 0 to 1, as said below
- w_out: bfloat16 [12288, 12288], P('col', 'row'), may hold values from -0.078125 to 0.078125
- bias_out: float32 [12288], P('row'), may hold values from -3 to 3
- mask_out: int32 [96, 96], P('col', 'row'), may hold values from 0 to 1, as said below
Outputs:
- mixed: bfloat16 [2048, 12288], P('col', 'row')
The draws below stay inside these ranges and needn't reach their ends.
Inputs may be any that keep to these rules, and one draw needn't show every extreme that they name: `mask_qkv`: 1 keeps a tile of 128 x 128 weights and 0 prunes it; the kept share differs between the blocks of tiles that the mesh places on different devices. `mask_out`: 1 keeps a tile of 128 x 128 weights and 0 prunes it; the kept share differs between the blocks of tiles that the mesh places on different devices.
All inputs are finite; a program needn't handle non-finite values.
Results may differ from the reference program's by a relative error of at most 0.023.
Values may be sent and summed in bfloat16 or wider, within the bound.
A program may use at most 64 MiB of HBM per device.

```python
import jax
import jax.numpy as jnp
from jax import lax

TILE = 128
HEAD_DIM = 128
HEADS = 96
D = 12288
TOKENS = 2048
N_ROW = 8
N_COL = 32


def tile_mask(key, leading, row_groups, col_groups):
    tiles = D // TILE
    level_key, keep_key = jax.random.split(key)
    levels = jax.random.randint(level_key, (leading, row_groups, col_groups), 1, 4)
    levels = jnp.repeat(jnp.repeat(levels, tiles // row_groups, axis=1), tiles // col_groups, axis=2)
    coins = jax.random.randint(keep_key, (leading, tiles, tiles), 0, 4)
    return (coins < levels).astype(jnp.int32)


def draw_mask_qkv(key, part):
    key = jax.random.fold_in(key, 11)
    return tile_mask(key, 3, N_ROW, N_COL)


def draw_mask_out(key, part):
    key = jax.random.fold_in(key, 23)
    return tile_mask(key, 1, N_COL, N_ROW)[0]


def feature_scales(key, lowest, highest):
    group = jnp.arange(D, dtype=jnp.int32) // (D // N_ROW)
    ratio = group.astype(jnp.float32) / jnp.float32(max(N_ROW - 1, 1))
    trend = lowest * jnp.exp(ratio * jnp.log(jnp.float32(highest / lowest)))
    jitter = jnp.exp(jax.random.uniform(key, (D,), jnp.float32, -0.22, 0.22))
    return trend * jitter


def draw_tokens(key, part):
    key = jax.random.fold_in(key, 41)
    scale_key, value_key = jax.random.split(key, 2)
    scales = feature_scales(scale_key, 0.5, 2.0)
    values = jax.random.normal(value_key, (TOKENS, D), jnp.float32) * scales[None, :]
    return jnp.clip(values, -12.0, 12.0).astype(jnp.bfloat16)


def draw_bias_qkv(key, part):
    key = jax.random.fold_in(key, 31)
    base_key, sign_key, pick_key = jax.random.split(key, 3)
    base = jnp.clip(0.5 * jax.random.normal(base_key, (3, D), jnp.float32), -3.0, 3.0)
    strengths = jnp.array([3.5, 4.5, 5.5], jnp.float32)
    ranks = jax.random.permutation(pick_key, HEADS)
    hot_count = max(3, HEADS // 8)
    chosen = jnp.sum(jnp.where((ranks % 3)[:, None] == jnp.arange(3)[None, :], strengths[None, :], 0.0), axis=1)
    level = jnp.where(ranks < hot_count, chosen, 0.0)
    level = jnp.repeat(level, HEAD_DIM)
    signs = jnp.where(jax.random.bernoulli(sign_key, 0.5, (D,)), 1.0, -1.0)
    shift = (level * signs).astype(jnp.float32)
    lift = jnp.stack([shift, shift, jnp.zeros_like(shift)])
    return (base + lift).astype(jnp.float32)


def block_scale(own_key, extent, cuts, least, top_value):
    def one(dim, parts):
        heights = jax.random.uniform(jax.random.fold_in(jax.random.fold_in(own_key, 6), dim), (parts,), jnp.float32, least / len(cuts), top_value / len(cuts))
        return jnp.repeat(jnp.exp(heights), extent[dim] // parts).reshape((-1,) + (1,) * (len(extent) - dim - 1))

    loudness = one(*cuts[0])
    for cut in cuts[1:]:
        loudness = loudness * one(*cut)
    return loudness


def noise(stream_key, dims, deviation, most, pieces=(), kind=jnp.bfloat16):
    values = jax.random.normal(stream_key, dims, jnp.float32) * deviation
    if len(pieces) > 0:
        values = block_scale(stream_key, dims, pieces, -0.22, 0.18) * values
    return jnp.clip(values, min=-most, max=most).astype(kind)


def setup_inputs(seed: int = 0) -> dict:
    arg_keys = jax.random.split(jax.random.key(seed), 10)
    return {
        "tokens": draw_tokens(jax.random.fold_in(arg_keys[9], 71), 0),
        "ln_gain": jnp.clip(1.0 + 0.15 * jax.random.normal(arg_keys[1], (D,), jnp.float32), 0.25, 1.75),
        "ln_bias": noise(arg_keys[2], (D,), 0.5, 3.0, ((0, 8),), jnp.float32),
        "w_qkv": noise(arg_keys[3], (3, D, D), (D // 2) ** -0.5, 0.078125, ((1, 8), (2, 32))),
        "bias_qkv": draw_bias_qkv(jax.random.fold_in(arg_keys[9], 71), 0),
        "mask_qkv": draw_mask_qkv(jax.random.fold_in(arg_keys[9], 71), 0),
        "w_out": noise(arg_keys[6], (D, D), (D // 2) ** -0.5, 0.078125, ((0, 32), (1, 8))),
        "bias_out": noise(arg_keys[7], (D,), 0.5, 3.0, ((0, 8),), jnp.float32),
        "mask_out": draw_mask_out(jax.random.fold_in(arg_keys[9], 71), 0),
    }


def expand(weights, mask):
    shape = weights.shape
    rows, cols = (mask.shape[-2], mask.shape[-1])
    tiled = weights.reshape(shape[:-2] + (rows, TILE, cols, TILE))
    keep = mask.astype(jnp.bfloat16)[..., :, None, :, None]
    return (tiled * keep).reshape(shape)

def reference(tokens, ln_gain, ln_bias, w_qkv, bias_qkv, mask_qkv, w_out, bias_out, mask_out):
    values = tokens.astype(jnp.float32)
    mean = lax.optimization_barrier(jnp.mean(values, axis=1, keepdims=True))
    var = lax.optimization_barrier(jnp.mean(values * values, axis=1, keepdims=True)) - mean * mean
    normed = ((values - mean) * lax.rsqrt(var + 1e-05) * ln_gain + ln_bias).astype(jnp.bfloat16)
    pruned_qkv = expand(w_qkv, mask_qkv)
    group = D // N_ROW

    def add_qkv(total, index):
        start = (index * group).astype(jnp.int32)
        rows = lax.dynamic_slice_in_dim(normed, start, group, 1).astype(jnp.float32)
        block = lax.dynamic_slice_in_dim(pruned_qkv, start, group, 1).astype(jnp.float32)
        part = jnp.einsum('td,kdf->tkf', rows, block)
        part = lax.optimization_barrier(part.astype(jnp.bfloat16)).astype(jnp.float32)
        return (total + part, None)
    start_qkv = jnp.zeros((TOKENS, 3, D), jnp.float32)
    summed, _ = lax.scan(add_qkv, start_qkv, jnp.arange(N_ROW, dtype=jnp.int32))
    qkv = (summed + bias_qkv[None]).astype(jnp.bfloat16)
    query = qkv[:, 0].reshape(TOKENS, HEADS, HEAD_DIM).transpose(1, 0, 2)
    keys = qkv[:, 1].reshape(TOKENS, HEADS, HEAD_DIM).transpose(1, 0, 2)
    vals = qkv[:, 2].reshape(TOKENS, HEADS, HEAD_DIM).transpose(1, 0, 2)
    position = jnp.arange(TOKENS, dtype=jnp.int32)
    allowed = position[None, :] <= position[:, None]

    def one_head(inputs):
        head_q, head_k, head_v = inputs
        scores = jnp.dot(head_q, head_k.T, preferred_element_type=jnp.float32) / jnp.sqrt(jnp.float32(HEAD_DIM))
        scores = jnp.where(allowed, scores, -jnp.inf)
        top = lax.optimization_barrier(jnp.max(scores, axis=1, keepdims=True))
        expo = jnp.exp(scores - top)
        weights = (expo / lax.optimization_barrier(jnp.sum(expo, axis=1, keepdims=True))).astype(jnp.bfloat16)
        return jnp.dot(weights, head_v, preferred_element_type=jnp.float32).astype(jnp.bfloat16)
    heads_out = lax.map(one_head, (query, keys, vals))
    context = heads_out.transpose(1, 0, 2).reshape(TOKENS, D)
    pruned_out = expand(w_out, mask_out)
    width = D // N_COL

    def add_out(total, index):
        start = (index * width).astype(jnp.int32)
        piece = lax.dynamic_slice_in_dim(context, start, width, 1)
        block = lax.dynamic_slice_in_dim(pruned_out, start, width, 0)
        part = jnp.dot(piece, block, preferred_element_type=jnp.float32)
        part = lax.optimization_barrier(part.astype(jnp.bfloat16)).astype(jnp.float32)
        return (total + part, None)
    start_out = jnp.zeros((TOKENS, D), jnp.float32)
    projected, _ = lax.scan(add_out, start_out, jnp.arange(N_COL, dtype=jnp.int32))
    return (values + projected + bias_out).astype(jnp.bfloat16)
```

```python
import functools

import jax
import jax.numpy as jnp
from jax import lax
from jax.experimental import pallas as pl
from jax.experimental.pallas import tpu as pltpu
from jax.sharding import PartitionSpec as P

BF, F32 = jnp.bfloat16, jnp.float32
HD = 128
D = 12288
FEAT = 1536
UNIT = 384
HALF, RING = 2, 4
LAST = None

ORDER_IN = ((0, 0), (1, 0), (0, 1), (0, 3), (1, 1), (1, 3), (0, 2), (1, 2))
ORDER_OUT = ((0, 2), (1, 2), (0, 1), (0, 3), (1, 1), (1, 3), (0, 0), (1, 0))


def kernel(tok, gain, lnb, wqkv, bqkv, mq, wout, bout, mo, out,
           X, W, WO, BH, stat, S, SB, SR, SUP, SDN, UR, HS, HR, Q, KV, C,
           PO, H1, U1, T, H2, U2, Z, ZS, ssem, rsem):
    r, c = lax.axis_index("row"), lax.axis_index("col")
    core, h = r % 2, r // 2
    y, zl, x = c % 4, (c // 4) % 2, c // 8
    sib = (r + 1 - 2 * core, c)
    hup, hdn, hop = ((r + 2) % 8, c), ((r + 6) % 8, c), ((r + 4) % 8, c)
    zpart = (r, c + 4 - 8 * zl)

    def at_x(k):
        return (r, ((x + k) % 4) * 8 + zl * 4 + y)

    def at_y(k):
        return (r, x * 8 + zl * 4 + (y + k) % 4)

    lead, minor = (x, y), (y, x)
    at_lead, at_minor = (at_x, at_y), (at_y, at_x)
    p = (h + 1 + 2 * zl) % 4

    ids = [0]
    pending = []

    def copy(src, dst, to):
        i = ids[0]
        ids[0] += 1
        return pltpu.make_async_remote_copy(
            src_ref=src, dst_ref=dst, send_sem=ssem.at[i], recv_sem=rsem.at[i],
            device_id=to, device_id_type=pl.DeviceIdType.MESH)

    def go(d, cond=None):
        pending.append((d, cond))
        d.start()
        return d

    partners = [sib, hup, hdn, hop, zpart, at_x(1), at_x(3), at_y(1), at_y(3)]
    bar = pltpu.get_barrier_semaphore()
    for d in partners:
        pl.semaphore_signal(bar, inc=1, device_id=d, device_id_type=pl.DeviceIdType.MESH)
    pl.semaphore_wait(bar, len(partners))

    vals = tok[...].astype(F32)
    s1 = jnp.sum(vals, axis=1, keepdims=True)
    s2 = jnp.sum(vals * vals, axis=1, keepdims=True)
    lane = lax.broadcasted_iota(jnp.int32, (64, 128), 1)
    stat[0] = jnp.where(lane < 64, s1, s2)
    d = go(copy(stat.at[0], stat.at[1], sib))
    d.wait_recv()
    stat[2] = stat[0] + stat[1]
    ds = [go(copy(stat.at[2], stat.at[3 + k], to)) for k, to in enumerate((hup, hdn, hop))]
    for d in ds:
        d.wait_recv()
    tot = (stat[2] + stat[3]) + (stat[4] + stat[5])
    mean = tot[:, 0:1] * (1.0 / D)
    var = tot[:, 64:65] * (1.0 / D) - mean * mean
    normed = ((vals - mean) * lax.rsqrt(var + 1e-5) * gain[...] + lnb[...]).astype(BF)
    for hf in range(2):
        X[hf, lead[hf], zl, minor[hf]] = normed[hf * 32:hf * 32 + 32]

    dz, d1 = [], {}
    for hf in range(2):
        ref = X.at[hf, lead[hf], zl, minor[hf]]
        dz.append(go(copy(ref, ref, zpart)))
        for k in (1, 3):
            d1[hf, 0, k] = go(copy(ref, ref, at_minor[hf](k)))

    for i in range(12):
        rows = slice(i * HD, i * HD + HD)
        for a in range(3):
            for k in range(3):
                w = wqkv[k, rows, a * HD:a * HD + HD].astype(F32) * mq[(k * 12 + i) * 3 + a].astype(F32)
                W[rows, a * UNIT + k * HD:a * UNIT + k * HD + HD] = w.astype(BF)
    for a in range(3):
        BH[a] = jnp.broadcast_to(
            jnp.concatenate([bqkv[k:k + 1, a * HD:a * HD + HD] for k in range(3)], axis=1), (8, UNIT))

    for hf in range(2):
        dz[hf].wait_recv()
        ref = X.at[hf, lead[hf], 1 - zl, minor[hf]]
        for k in (1, 3):
            d1[hf, 1, k] = go(copy(ref, ref, at_minor[hf](k)))
    df = {}
    for g in range(2):
        gz = zl if g == 0 else 1 - zl
        step = 1 + 2 * gz
        for hf in range(2):
            for k in (1, 3):
                d1[hf, g, k].wait_recv()
            ref = X.at[hf, lead[hf], gz, (minor[hf] + 4 - step) % 4]
            df[hf, g] = go(copy(ref, ref, at_minor[hf](step)))
    d2 = {}
    for hf in range(2):
        for g in range(2):
            df[hf, g].wait_recv()
    for g in range(2):
        for hf in range(2):
            for k, gg in ((1, g), (3, 1 - g)):
                ref = X.at[hf, lead[hf], gg]
                d2[hf, k, gg] = go(copy(ref, ref, at_lead[hf](k)))

    def forward_lead(hf):
        for k, gg in ((1, 0), (3, 1)):
            d2[hf, k, gg].wait_recv()
            ref = X.at[hf, (lead[hf] + 4 - k) % 4, gg]
            d2[hf, 2, gg] = go(copy(ref, ref, at_lead[hf](k)))

    dsib, dup, ddn, dhup, dhdn, dkv = {}, {}, {}, {}, {}, {}

    def stage_m(t):
        hf, k = ORDER_IN[t]
        l = (lead[hf] + k) % 4
        if k in (1, 3):
            for gg in range(2):
                if (4 - k, gg) not in ((1, 0), (3, 1)):
                    d2[hf, 4 - k, gg].wait_recv()
        elif k == 2:
            for gg in range(2):
                d2[hf, 2, gg].wait_recv()
        rows = jnp.concatenate(
            [X[hf, l, core].reshape(128, FEAT), X[hf, l, 1 - core].reshape(128, FEAT)], axis=0)
        acc = jnp.dot(rows, W[...], preferred_element_type=F32)
        for a in range(3):
            S[t, a] = acc[:128, a * UNIT:a * UNIT + UNIT]
            SB[t, a] = acc[128:, a * UNIT:a * UNIT + UNIT].astype(BF)
        dsib[t] = go(copy(SB.at[t], SR.at[t], sib))

    a_up = jnp.where(p == 1, 1, jnp.where(p == 2, 2, 0))
    a_dn = jnp.where(p == 2, 0, jnp.where(p == 3, 1, 2))

    def stage_e(t):
        dsib[t].wait_recv()
        for a in range(3):
            S[t, a] = S[t, a] + SR[t, a].astype(F32)
        dup[t] = copy(SUP.at[t], UR.at[0, t], hup)
        ddn[t] = copy(SDN.at[t], UR.at[1, t], hdn)
        dhup[t] = copy(HS.at[0, t], HR.at[0, t], hup)
        dhdn[t] = copy(HS.at[1, t], HR.at[1, t], hdn)
        pending.extend([(dup[t], None), (ddn[t], None), (dhup[t], p == 0), (dhdn[t], p == 0)])

        @pl.when(p >= 2)
        def _():
            SUP[t] = S[t, a_up].astype(BF)
            dup[t].start()

        @pl.when((p == 1) | (p == 2))
        def _():
            SDN[t] = S[t, a_dn].astype(BF)
            ddn[t].start()

        @pl.when(p == 0)
        def _():
            HS[0, t] = S[t, 1, 0:64].astype(BF)
            dhup[t].start()
            HS[1, t] = S[t, 1, 64:128].astype(BF)
            dhdn[t].start()

    def stage_f(t):
        @pl.when(p == 0)
        def _():
            dup[t].wait_recv()
            SUP[t] = (S[t, 0] + UR[0, t].astype(F32)).astype(BF)
            dup[t].start()
            ddn[t].wait_recv()
            SDN[t] = (S[t, 2] + UR[1, t].astype(F32)).astype(BF)
            ddn[t].start()

        @pl.when(p == 1)
        def _():
            SUP[t, 64:128] = S[t, 1, 64:128].astype(BF)
            dhup[t].wait_recv()
            SUP[t, 0:64] = (S[t, 1, 0:64] + HR[0, t].astype(F32)).astype(BF)
            dup[t].start()

        @pl.when(p == 3)
        def _():
            SDN[t, 0:64] = S[t, 1, 0:64].astype(BF)
            dhdn[t].wait_recv()
            SDN[t, 64:128] = (S[t, 1, 64:128] + HR[1, t].astype(F32)).astype(BF)
            ddn[t].start()

    def stage_g(t):
        hf, k = ORDER_IN[t]
        l = (lead[hf] + k) % 4
        ref = KV.at[:, l, core, :, 0] if hf == 0 else KV.at[:, :, core, l, 1]
        dkv[t] = copy(ref, ref, sib)
        pending.append((dkv[t], p > 0))

        @pl.when(p > 0)
        def _():
            dup[t].wait_recv()
            ddn[t].wait_recv()
            total = S[t, p - 1] + UR[0, t].astype(F32) + UR[1, t].astype(F32) + BH[p - 1][0:1]
            total = total.astype(BF)
            for m in range(4):
                at = (l, m) if hf == 0 else (m, l)
                part = total[m * 32:m * 32 + 32]
                Q[at[0], at[1], hf] = part[:, 0:HD]
                KV[0, at[0], core, at[1], hf] = part[:, HD:2 * HD]
                KV[1, at[0], core, at[1], hf] = part[:, 2 * HD:]
            dkv[t].start()

    stage_m(0)
    stage_m(1)
    stage_e(0)
    stage_e(1)
    stage_f(0)
    stage_f(1)
    forward_lead(0)
    forward_lead(1)
    for i in range(3):
        for j in range(12):
            blk = (slice(i * HD, i * HD + HD), slice(j * HD, j * HD + HD))
            WO[blk] = (wout[blk].astype(F32) * mo[i * 12 + j].astype(F32)).astype(BF)
    stage_g(0)
    stage_g(1)
    for t in range(2, 8):
        stage_m(t)
        if t >= 3:
            stage_e(t - 1)
        if t >= 4:
            stage_f(t - 2)
        if t >= 5:
            stage_g(t - 3)
    stage_e(7)
    stage_f(6)
    stage_g(5)
    stage_f(7)
    stage_g(6)
    stage_g(7)

    a_own = jnp.where(p > 0, p - 1, 0)

    @pl.when(p > 0)
    def _():
        for t in range(8):
            dkv[t].wait_recv()
        scale = 1.4426950408889634 / (HD ** 0.5)
        for b in range(4):
            n = 512 * (b + 1)
            q = Q[b].reshape(256, HD)
            keys = KV[0, 0:b + 1].reshape(n, HD)
            values = KV[1, 0:b + 1].reshape(n, HD)
            s = lax.dot_general(q, keys, (((1,), (1,)), ((), ())), preferred_element_type=F32)
            qpos = lax.broadcasted_iota(jnp.int32, (256, 512), 0) + core * 256
            kpos = lax.broadcasted_iota(jnp.int32, (256, 512), 1)
            diag = jnp.where(kpos <= qpos, s[:, n - 512:], -jnp.inf)
            s = diag if b == 0 else jnp.concatenate([s[:, :n - 512], diag], axis=1)
            top = jnp.max(s, axis=1, keepdims=True)
            e = jnp.exp2((s - top) * scale)
            inv = 1.0 / jnp.sum(e, axis=1, keepdims=True)
            ctx = jnp.dot((e * inv).astype(BF), values, preferred_element_type=F32).astype(BF)
            ctx = ctx.reshape(4, 2, 32, HD)
            for m in range(4):
                C[0, b, core, a_own, m] = ctx[m, 0]
                C[1, m, core, a_own, b] = ctx[m, 1]

    a_prev = (p + 2) % 4
    a_next = p
    a_opp = (p + 1) % 4
    has_prev, has_next, has_opp = p != 1, p != 3, p != 2
    a_prev, a_next, a_opp = a_prev % 3, a_next % 3, a_opp % 3
    cup, cdn, fup, fdn, cs = {}, {}, {}, {}, {}
    for t in range(8):
        hf, k = ORDER_OUT[t]
        l = (lead[hf] + k) % 4
        ref = C.at[hf, l, core, a_own]
        cup[t], cdn[t] = copy(ref, ref, hup), copy(ref, ref, hdn)
        pending.extend([(cup[t], p > 0), (cdn[t], p > 0)])

        @pl.when(p > 0)
        def _():
            cup[t].start()
            cdn[t].start()

    def stage_a(t):
        hf, k = ORDER_OUT[t]
        l = (lead[hf] + k) % 4
        ref = C.at[hf, l, core, a_prev, 0:2]
        fup[t] = copy(ref, ref, hup)
        ref = C.at[hf, l, core, a_next, 2:4]
        fdn[t] = copy(ref, ref, hdn)
        pending.extend([(fup[t], has_prev), (fdn[t], has_next)])

        @pl.when(has_prev)
        def _():
            cup[t].wait_recv()
            fup[t].start()

        @pl.when(has_next)
        def _():
            cdn[t].wait_recv()
            fdn[t].start()

    def stage_b(t):
        hf, k = ORDER_OUT[t]
        l = (lead[hf] + k) % 4

        @pl.when(has_opp)
        def _():
            fup[t].wait_recv()
            fdn[t].wait_recv()
        ref = C.at[hf, l, core]
        cs[t] = go(copy(ref, ref, sib))

    e1, u1 = {}, {}

    def stage_c(t):
        hf, k = ORDER_OUT[t]
        l = (lead[hf] + k) % 4
        cs[t].wait_recv()
        rows = jnp.concatenate(
            [jnp.concatenate([C[hf, l, g, a].reshape(128, HD) for a in range(3)], axis=1)
             for g in range(2)], axis=0)
        acc = jnp.dot(rows, WO[...], preferred_element_type=F32)
        lo, hi = acc[:128].reshape(4, 32, FEAT), acc[128:].reshape(4, 32, FEAT)
        if k == 2:
            PO[t, 0] = lo.astype(BF)
            e1[hf, 0] = go(copy(PO.at[t, 0], H1.at[hf, 0], at_lead[hf](1)))
            PO[t, 1] = hi.astype(BF)
            e1[hf, 1] = go(copy(PO.at[t, 1], H1.at[hf, 1], at_lead[hf](3)))
        elif k == 1:
            PO[t, 1] = hi.astype(BF)
            u1[hf, 0, 1] = go(copy(PO.at[t, 1], U1.at[hf, 0, 1], at_lead[hf](1)))
            e1[hf, 0].wait_recv()
            PO[t, 0] = (lo + H1[hf, 0].astype(F32)).astype(BF)
            u1[hf, 0, 0] = go(copy(PO.at[t, 0], U1.at[hf, 0, 0], at_lead[hf](1)))
        elif k == 3:
            PO[t, 0] = lo.astype(BF)
            u1[hf, 1, 0] = go(copy(PO.at[t, 0], U1.at[hf, 1, 0], at_lead[hf](3)))
            e1[hf, 1].wait_recv()
            PO[t, 1] = (hi + H1[hf, 1].astype(F32)).astype(BF)
            u1[hf, 1, 1] = go(copy(PO.at[t, 1], U1.at[hf, 1, 1], at_lead[hf](3)))
        else:
            T[hf, 0] = lo
            T[hf, 1] = hi

    for t in range(10):
        if t < 8:
            stage_a(t)
        if 1 <= t < 9:
            stage_b(t - 1)
        if t >= 2:
            stage_c(t - 2)

    e2, u2, ez = {}, {}, {}
    for hf in range(2):
        m, to = minor[hf], at_minor[hf]
        m2, mp, mm = (m + 2) % 4, (m + 1) % 4, (m + 3) % 4
        for dr in range(2):
            for g in range(2):
                u1[hf, dr, g].wait_recv()
        for g in range(2):
            T[hf, g] = T[hf, g] + U1[hf, 0, g].astype(F32) + U1[hf, 1, g].astype(F32)
        ZS[hf, 0, 0] = T[hf, 0, m2].astype(BF)
        ZS[hf, 0, 1] = T[hf, 1, m2].astype(BF)
        e2[hf, 0] = go(copy(ZS.at[hf, 0, 0], H2.at[hf, 0], to(1)))
        e2[hf, 1] = go(copy(ZS.at[hf, 0, 1], H2.at[hf, 1], to(3)))
        ZS[hf, 1, 1] = T[hf, 1, mp].astype(BF)
        ZS[hf, 2, 0] = T[hf, 0, mm].astype(BF)
        u2[hf, 0, 1] = go(copy(ZS.at[hf, 1, 1], U2.at[hf, 0, 1], to(1)))
        u2[hf, 1, 0] = go(copy(ZS.at[hf, 2, 0], U2.at[hf, 1, 0], to(3)))
    for hf in range(2):
        m, to = minor[hf], at_minor[hf]
        mp, mm = (m + 1) % 4, (m + 3) % 4
        e2[hf, 0].wait_recv()
        ZS[hf, 1, 0] = (T[hf, 0, mp] + H2[hf, 0].astype(F32)).astype(BF)
        u2[hf, 0, 0] = go(copy(ZS.at[hf, 1, 0], U2.at[hf, 0, 0], to(1)))
        e2[hf, 1].wait_recv()
        ZS[hf, 2, 1] = (T[hf, 1, mm] + H2[hf, 1].astype(F32)).astype(BF)
        u2[hf, 1, 1] = go(copy(ZS.at[hf, 2, 1], U2.at[hf, 1, 1], to(3)))
    for hf in range(2):
        m = minor[hf]
        for dr in range(2):
            for g in range(2):
                u2[hf, dr, g].wait_recv()
        g = 1 - zl
        ZS[hf, 3, 0] = (T[hf, g, m] + U2[hf, 0, g].astype(F32) + U2[hf, 1, g].astype(F32)).astype(BF)
        ez[hf] = go(copy(ZS.at[hf, 3, 0], Z.at[hf], zpart))
    for hf in range(2):
        m = minor[hf]
        rows = slice(hf * 32, hf * 32 + 32)
        own = T[hf, zl, m] + U2[hf, 0, zl].astype(F32) + U2[hf, 1, zl].astype(F32)
        own = own + tok[rows].astype(F32) + bout[...]
        ez[hf].wait_recv()
        out[rows] = (own + Z[hf].astype(F32)).astype(BF)

    for d, cond in pending:
        if cond is None:
            d.wait_send()
        else:
            pl.when(cond)(d.wait_send)


SCRATCH = [
    pltpu.VMEM((2, 4, 2, 4, 32, FEAT), BF),
    pltpu.VMEM((FEAT, 3 * UNIT), BF),
    pltpu.VMEM((UNIT, FEAT), BF),
    pltpu.VMEM((3, 8, UNIT), F32),
    pltpu.VMEM((6, 64, 128), F32),
    pltpu.VMEM((8, 3, 128, UNIT), F32),
    pltpu.VMEM((8, 3, 128, UNIT), BF),
    pltpu.VMEM((8, 3, 128, UNIT), BF),
    pltpu.VMEM((8, 128, UNIT), BF),
    pltpu.VMEM((8, 128, UNIT), BF),
    pltpu.VMEM((2, 8, 128, UNIT), BF),
    pltpu.VMEM((2, 8, 64, UNIT), BF),
    pltpu.VMEM((2, 8, 64, UNIT), BF),
    pltpu.VMEM((4, 4, 2, 32, HD), BF),
    pltpu.VMEM((2, 4, 2, 4, 2, 32, HD), BF),
    pltpu.VMEM((2, 4, 2, 3, 4, 32, HD), BF),
    pltpu.VMEM((6, 2, 4, 32, FEAT), BF),
    pltpu.VMEM((2, 2, 4, 32, FEAT), BF),
    pltpu.VMEM((2, 2, 2, 4, 32, FEAT), BF),
    pltpu.VMEM((2, 2, 4, 32, FEAT), F32),
    pltpu.VMEM((2, 2, 32, FEAT), BF),
    pltpu.VMEM((2, 2, 2, 32, FEAT), BF),
    pltpu.VMEM((2, 32, FEAT), BF),
    pltpu.VMEM((2, 4, 2, 32, FEAT), BF),
    pltpu.SemaphoreType.DMA((256,)),
    pltpu.SemaphoreType.DMA((256,)),
]


def body(tokens, ln_gain, ln_bias, w_qkv, bias_qkv, mask_qkv, w_out, bias_out, mask_out):
    vm = pl.BlockSpec(memory_space=pltpu.VMEM)
    sm = pl.BlockSpec(memory_space=pltpu.SMEM)
    return pl.pallas_call(
        kernel,
        out_shape=jax.ShapeDtypeStruct((64, FEAT), BF),
        in_specs=[vm, vm, vm, vm, vm, sm, vm, vm, sm],
        out_specs=vm,
        scratch_shapes=SCRATCH,
        compiler_params=pltpu.CompilerParams(
            collective_id=0, has_side_effects=True, vmem_limit_bytes=60 * 1024 * 1024),
    )(tokens, ln_gain.reshape(1, FEAT), ln_bias.reshape(1, FEAT), w_qkv, bias_qkv,
      mask_qkv.reshape(-1), w_out, bias_out.reshape(1, FEAT), mask_out.reshape(-1))


def solution(mesh):
    placed = (
        P("col", "row"),
        P("row"),
        P("row"),
        P(None, "row", "col"),
        P(None, "col"),
        P(None, "row", "col"),
        P("col", "row"),
        P("row"),
        P("col", "row"),
    )
    return jax.shard_map(
        body, mesh=mesh, in_specs=placed, out_specs=P("col", "row"), check_vma=False
    )
```

```python
import functools

import jax
import jax.numpy as jnp
from jax import lax
from jax.experimental import pallas as pl
from jax.experimental.pallas import tpu as pltpu
from jax.sharding import PartitionSpec as P

BF, F32 = jnp.bfloat16, jnp.float32
HD = 128
D = 12288
FEAT = 1536
UNIT = 384
HALF, RING = 2, 4

ORDER_IN = tuple((hf, k0, k1, m, 2) for k0, k1 in ((0, 0), (3, 1), (1, 3), (2, 2))
                 for m in (0, 2) for hf in (0, 1))
OFF = [32 * sum(q[4] for q in ORDER_IN[:t]) for t in range(len(ORDER_IN))]
PIECES = len(ORDER_IN)
SCHEDULE = (
    "M0", "M1", "E0", "E1", "M2", "M3", "E2", "E3", "F0", "F1", "P", "F2", "F3", "W", "M4", "M5", "E4", "E5", "M6", "M7", "E6", "E7", "F4", "F5", "M8", "M9", "E8",
    "E9", "F6", "F7", "M10", "M11", "E10", "E11", "F8", "F9", "M12", "M13", "E12", "E13", "F10", "F11", "M14", "M15", "E14", "E15", "F12", "F13",
    "F14", "F15", "G0", "G1", "G2", "G3", "G4", "G5", "G6", "G7", "G8", "G9", "G10", "G11", "G12", "G13", "G14", "G15",
)
SCHEDULE_OUT = (
    "S0", "S1", "B0", "S2", "B1", "S3", "C0", "S4", "C1", "S5", "B2", "C2", "B3", "C3", "S6", "S7",
    "B4", "C4", "B5", "C5", "B6", "B7", "D0", "D1", "D2", "D3", "C6", "C7",
)
ORDER_OUT = ((0, 2), (1, 2), (0, 1), (0, 3), (1, 1), (1, 3), (0, 0), (1, 0))


def kernel(tok, gain, lnb, wqkv_hbm, bqkv, mq, wout_hbm, bout, mo, out,
           wqkv, wout, RZ, X, W, WO, BH, stat, S, SB, SR, SUP, SDN, UR, HS, HR, Q, KV, C,
           PO, H1, U1, T, H2, U2, Z, ZS, ssem, rsem, lsem):
    r, c = lax.axis_index("row"), lax.axis_index("col")
    core, h = r % 2, r // 2
    y, zl, x = c % 4, (c // 4) % 2, c // 8
    sib = (r + 1 - 2 * core, c)
    hup, hdn, hop = ((r + 2) % 8, c), ((r + 6) % 8, c), ((r + 4) % 8, c)
    zpart = (r, c + 4 - 8 * zl)

    def at_x(k):
        return (r, ((x + k) % 4) * 8 + zl * 4 + y)

    def at_y(k):
        return (r, x * 8 + zl * 4 + (y + k) % 4)

    lead, minor = (x, y), (y, x)
    at_lead, at_minor = (at_x, at_y), (at_y, at_x)
    p = (h + 1 + 2 * zl) % 4

    ids = [0]
    pending = []

    def copy(src, dst, to):
        i = ids[0]
        ids[0] += 1
        return pltpu.make_async_remote_copy(
            src_ref=src, dst_ref=dst, send_sem=ssem.at[i], recv_sem=rsem.at[i],
            device_id=to, device_id_type=pl.DeviceIdType.MESH)

    def go(d, cond=None):
        pending.append((d, cond))
        d.start()
        return d

    load_w = pltpu.make_async_copy(wqkv_hbm, wqkv, lsem.at[0])
    load_w.start()
    load_o = pltpu.make_async_copy(wout_hbm, wout, lsem.at[1])
    load_o.start()
    peers = [((r + k) % 8, c) for k in range(1, 8)]
    partners = peers + [zpart, at_x(1), at_x(3), at_y(1), at_y(3)]
    bar = pltpu.get_barrier_semaphore()
    for d in partners:
        pl.semaphore_signal(bar, inc=1, device_id=d, device_id_type=pl.DeviceIdType.MESH)

    vals = tok[...].astype(F32)
    s1 = jnp.sum(vals, axis=1, keepdims=True)
    s2 = jnp.sum(vals * vals, axis=1, keepdims=True)
    lane = lax.broadcasted_iota(jnp.int32, (64, 128), 1)
    line = lax.broadcasted_iota(jnp.int32, (64, 128), 0)
    packed = jnp.where(lane == line, s1, 0.0) + jnp.where(lane == line + 64, s2, 0.0)
    stat[0] = jnp.broadcast_to(jnp.sum(packed, axis=0, keepdims=True), (8, 128))
    pl.semaphore_wait(bar, len(partners))
    ds = [go(copy(stat.at[0], stat.at[k + 1], to)) for k, to in enumerate(peers)]
    raw = go(copy(tok, RZ, zpart))
    tot = stat[0]
    for k, d in enumerate(ds):
        d.wait_recv()
        tot = tot + stat[k + 1]
    stat[8] = tot
    dt = go(copy(stat.at[8], stat.at[9], zpart))

    def normalise(values, sums, gz):
        sums = sums[0:1]
        mean = jnp.sum(jnp.where(lane == line, sums, 0.0), axis=1, keepdims=True) * (1.0 / D)
        square = jnp.sum(jnp.where(lane == line + 64, sums, 0.0), axis=1, keepdims=True) * (1.0 / D)
        var = square - mean * mean
        normed = (values - mean) * lax.rsqrt(var + 1e-5) * gain[...].reshape(1, FEAT) + lnb[...].reshape(1, FEAT)
        normed = normed.astype(BF)
        for hf in range(2):
            X[hf, lead[hf], gz, minor[hf]] = normed[hf * 32:hf * 32 + 32]

    d1 = {}

    def send_minor(g):
        for hf in range(2):
            ref = X.at[hf, lead[hf], zl if g == 0 else 1 - zl, minor[hf]]
            for k in (1, 3):
                d1[hf, g, k] = go(copy(ref, ref, at_minor[hf](k)))

    normalise(vals, tot, zl)
    send_minor(0)
    raw.wait_recv()
    dt.wait_recv()
    normalise(RZ[...].astype(F32), stat[9], 1 - zl)
    send_minor(1)

    load_w.wait()

    def prune_qkv(part):
        for i in part:
            rows = slice(i * HD, i * HD + HD)
            for a in range(3):
                for k in range(3):
                    w = wqkv[k, rows, a * HD:a * HD + HD].astype(F32) * mq[k, a, i].astype(F32)
                    W[rows, a * UNIT + k * HD:a * UNIT + k * HD + HD] = w.astype(BF)

    df = {}
    for g in range(2):
        prune_qkv(range(6 * g, 6 * g + 6))
        gz = zl if g == 0 else 1 - zl
        step = 1 + 2 * gz
        for hf in range(2):
            for k in (1, 3):
                d1[hf, g, k].wait_recv()
            ref = X.at[hf, lead[hf], gz, (minor[hf] + 4 - step) % 4]
            df[hf, g] = go(copy(ref, ref, at_minor[hf](step)))
    for a in range(3):
        BH[a] = jnp.broadcast_to(
            jnp.concatenate([bqkv[k:k + 1, a * HD:a * HD + HD] for k in range(3)], axis=1), (8, UNIT))
    d2 = {}
    for hf in range(2):
        for g in range(2):
            df[hf, g].wait_recv()
    for g in range(2):
        for hf in range(2):
            for k, gg in ((1, g), (3, 1 - g)):
                ref = X.at[hf, lead[hf], gg]
                d2[hf, k, gg] = go(copy(ref, ref, at_lead[hf](k)))

    def forward_lead(hf):
        for k, gg in ((1, 0), (3, 1)):
            d2[hf, k, gg].wait_recv()
            ref = X.at[hf, (lead[hf] + 4 - k) % 4, gg]
            d2[hf, 2, gg] = go(copy(ref, ref, at_lead[hf](k)))

    dsib, dup, ddn, dhup, dhdn, dkv = {}, {}, {}, {}, {}, {}

    waited = {(h_, k_, g_) for h_ in range(2) for k_, g_ in ((1, 0), (3, 1))}

    def span(t):
        n = 32 * ORDER_IN[t][4]
        return n, slice(OFF[t], OFF[t] + n), pl.ds(OFF[t], n), pl.ds(OFF[t] // 2, n // 2)

    def stage_m(t):
        hf, k0, k1, m0, mn = ORDER_IN[t]
        n, at, ds_, _ = span(t)
        for k, gg in ((k0, 0), (k1, 1)):
            if k and (hf, 4 - k, gg) not in waited:
                d2[hf, 4 - k, gg].wait_recv()
                waited.add((hf, 4 - k, gg))
        l = [(lead[hf] + k) % 4 for k in (k0, k1)]
        own, other = jnp.where(core == 0, l[0], l[1]), jnp.where(core == 0, l[1], l[0])
        rows = jnp.concatenate(
            [X[hf, own, core, m0:m0 + mn].reshape(n, FEAT),
             X[hf, other, 1 - core, m0:m0 + mn].reshape(n, FEAT)], axis=0)
        acc = jnp.dot(rows, W[...], preferred_element_type=F32)
        for a in range(3):
            S[a, at] = acc[:n, a * UNIT:a * UNIT + UNIT]
            SB[a, at] = acc[n:, a * UNIT:a * UNIT + UNIT].astype(BF)
        dsib[t] = go(copy(SB.at[:, ds_], SR.at[:, ds_], sib))

    a_up = jnp.where(p == 1, 1, jnp.where(p == 2, 2, 0))
    a_dn = jnp.where(p == 2, 0, jnp.where(p == 3, 1, 2))

    def stage_e(t):
        n, at, ds_, hs_ = span(t)
        mid, low = OFF[t] + n // 2, slice(OFF[t] // 2, OFF[t] // 2 + n // 2)
        dsib[t].wait_recv()
        for a in range(3):
            S[a, at] = S[a, at] + SR[a, at].astype(F32)
        dup[t] = copy(SUP.at[ds_], UR.at[0, ds_], hup)
        ddn[t] = copy(SDN.at[ds_], UR.at[1, ds_], hdn)
        dhup[t] = copy(HS.at[0, hs_], HR.at[0, hs_], hup)
        dhdn[t] = copy(HS.at[1, hs_], HR.at[1, hs_], hdn)
        pending.extend([(dup[t], None), (ddn[t], None), (dhup[t], p == 0), (dhdn[t], p == 0)])

        @pl.when(p >= 2)
        def _():
            SUP[at] = S[a_up, at].astype(BF)
            dup[t].start()

        @pl.when((p == 1) | (p == 2))
        def _():
            SDN[at] = S[a_dn, at].astype(BF)
            ddn[t].start()

        @pl.when(p == 0)
        def _():
            HS[0, low] = S[1, OFF[t]:mid].astype(BF)
            dhup[t].start()
            HS[1, low] = S[1, mid:OFF[t] + n].astype(BF)
            dhdn[t].start()

    def stage_f(t):
        n, at, _, _ = span(t)
        mid, low = OFF[t] + n // 2, slice(OFF[t] // 2, OFF[t] // 2 + n // 2)
        first, second = slice(OFF[t], mid), slice(mid, OFF[t] + n)

        @pl.when(p == 0)
        def _():
            dup[t].wait_recv()
            SUP[at] = (S[0, at] + UR[0, at].astype(F32)).astype(BF)
            dup[t].start()
            ddn[t].wait_recv()
            SDN[at] = (S[2, at] + UR[1, at].astype(F32)).astype(BF)
            ddn[t].start()

        @pl.when(p == 1)
        def _():
            SUP[second] = S[1, second].astype(BF)
            dhup[t].wait_recv()
            SUP[first] = (S[1, first] + HR[0, low].astype(F32)).astype(BF)
            dup[t].start()

        @pl.when(p == 3)
        def _():
            SDN[first] = S[1, first].astype(BF)
            dhdn[t].wait_recv()
            SDN[second] = (S[1, second] + HR[1, low].astype(F32)).astype(BF)
            ddn[t].start()

    def stage_g(t):
        hf, k0, k1, m0, mn = ORDER_IN[t]
        _, at, _, _ = span(t)
        l = (lead[hf] + jnp.where(core == 0, k0, k1)) % 4
        ms = pl.ds(m0, mn)
        ref = KV.at[:, l, core, ms, 0] if hf == 0 else KV.at[:, ms, core, l, 1]
        dkv[t] = copy(ref, ref, sib)
        pending.append((dkv[t], p > 0))

        @pl.when(p > 0)
        def _():
            dup[t].wait_recv()
            ddn[t].wait_recv()
            total = S[p - 1, at] + UR[0, at].astype(F32) + UR[1, at].astype(F32) + BH[p - 1][0:1]
            total = total.astype(BF)
            for m in range(mn):
                where = (l, m0 + m) if hf == 0 else (m0 + m, l)
                part = total[m * 32:m * 32 + 32]
                Q[where[0], where[1], hf] = part[:, 0:HD]
                KV[0, where[0], core, where[1], hf] = part[:, HD:2 * HD]
                KV[1, where[0], core, where[1], hf] = part[:, 2 * HD:]
            dkv[t].start()

    def prune_out():
        load_o.wait()
        for i in range(3):
            for j in range(12):
                blk = (slice(i * HD, i * HD + HD), slice(j * HD, j * HD + HD))
                WO[blk] = (wout[blk].astype(F32) * mo[i, j].astype(F32)).astype(BF)

    def pass_on(t):
        forward_lead(0)
        forward_lead(1)

    stages = dict(M=stage_m, E=stage_e, F=stage_f, G=stage_g, W=pass_on, P=lambda t: prune_out())
    for word in SCHEDULE:
        stages[word[0]](int(word[1:] or 0))

    a_own = jnp.where(p > 0, p - 1, 0)

    @pl.when(p > 0)
    def _():
        for t in range(PIECES):
            dkv[t].wait_recv()
        scale = 1.4426950408889634 / (HD ** 0.5)
        for b in range(4):
            n = 512 * (b + 1)
            q = Q[b].reshape(256, HD)
            keys = KV[0, 0:b + 1].reshape(n, HD)
            values = KV[1, 0:b + 1].reshape(n, HD)
            s = lax.dot_general(q, keys, (((1,), (1,)), ((), ())), preferred_element_type=F32)
            qpos = lax.broadcasted_iota(jnp.int32, (256, 512), 0) + core * 256
            kpos = lax.broadcasted_iota(jnp.int32, (256, 512), 1)
            diag = jnp.where(kpos <= qpos, s[:, n - 512:], -jnp.inf)
            s = diag if b == 0 else jnp.concatenate([s[:, :n - 512], diag], axis=1)
            top = jnp.max(s, axis=1, keepdims=True)
            e = jnp.exp2((s - top) * scale)
            inv = 1.0 / jnp.sum(e, axis=1, keepdims=True)
            ctx = jnp.dot((e * inv).astype(BF), values, preferred_element_type=F32).astype(BF)
            ctx = ctx.reshape(4, 2, 32, HD)
            for m in range(4):
                C[0, b, core, a_own, m] = ctx[m, 0]
                C[1, m, core, a_own, b] = ctx[m, 1]

    dctx, cs = {}, {}

    def send_ctx(t):
        hf, k = ORDER_OUT[t]
        ref = C.at[hf, (lead[hf] + k) % 4, core, a_own]
        dctx[t] = [copy(ref, ref, to) for to in (hup, hdn, hop)]
        pending.extend([(d, p > 0) for d in dctx[t]])

        @pl.when(p > 0)
        def _():
            for d in dctx[t]:
                d.start()

    def stage_b(t):
        hf, k = ORDER_OUT[t]
        for d, cond in zip(dctx[t], (p != 1, p != 3, p != 2)):
            pl.when(cond)(d.wait_recv)
        ref = C.at[hf, (lead[hf] + k) % 4, core]
        cs[t] = go(copy(ref, ref, sib))

    e1, u1 = {}, {}

    def stage_c(t):
        hf, k = ORDER_OUT[t]
        l = (lead[hf] + k) % 4
        cs[t].wait_recv()
        rows = jnp.concatenate(
            [jnp.concatenate([C[hf, l, g, a].reshape(128, HD) for a in range(3)], axis=1)
             for g in range(2)], axis=0)
        acc = jnp.dot(rows, WO[...], preferred_element_type=F32)
        lo, hi = acc[:128].reshape(4, 32, FEAT), acc[128:].reshape(4, 32, FEAT)
        if k == 2:
            PO[t, 0] = lo.astype(BF)
            e1[hf, 0] = go(copy(PO.at[t, 0], H1.at[hf, 0], at_lead[hf](1)))
            PO[t, 1] = hi.astype(BF)
            e1[hf, 1] = go(copy(PO.at[t, 1], H1.at[hf, 1], at_lead[hf](3)))
        elif k == 1:
            PO[t, 1] = hi.astype(BF)
            u1[hf, 0, 1] = go(copy(PO.at[t, 1], U1.at[hf, 0, 1], at_lead[hf](1)))
            PO[t, 0] = lo.astype(BF)
        elif k == 3:
            PO[t, 0] = lo.astype(BF)
            u1[hf, 1, 0] = go(copy(PO.at[t, 0], U1.at[hf, 1, 0], at_lead[hf](3)))
            PO[t, 1] = hi.astype(BF)
        else:
            T[hf, 0] = lo
            T[hf, 1] = hi

    def stage_d(hf, g):
        k = 1 if g == 0 else 3
        t = ORDER_OUT.index((hf, k))
        e1[hf, g].wait_recv()
        PO[t, g] = (PO[t, g].astype(F32) + H1[hf, g].astype(F32)).astype(BF)
        u1[hf, g, g] = go(copy(PO.at[t, g], U1.at[hf, g, g], at_lead[hf](k)))

    stages = dict(S=send_ctx, B=stage_b, C=stage_c, D=lambda i: stage_d(i // 2, i % 2))
    for word in SCHEDULE_OUT:
        stages[word[0]](int(word[1:]))

    e2, u2, ez = {}, {}, {}
    for hf in range(2):
        m, to = minor[hf], at_minor[hf]
        m2, mp, mm = (m + 2) % 4, (m + 1) % 4, (m + 3) % 4
        for dr in range(2):
            for g in range(2):
                u1[hf, dr, g].wait_recv()

        def add(g, mi):
            t_ = T[hf, g, mi] + U1[hf, 0, g, mi].astype(F32) + U1[hf, 1, g, mi].astype(F32)
            T[hf, g, mi] = t_
            return t_.astype(BF)

        ZS[hf, 0, 0] = add(0, m2)
        e2[hf, 0] = go(copy(ZS.at[hf, 0, 0], H2.at[hf, 0], to(1)))
        ZS[hf, 0, 1] = add(1, m2)
        e2[hf, 1] = go(copy(ZS.at[hf, 0, 1], H2.at[hf, 1], to(3)))
        ZS[hf, 1, 1] = add(1, mp)
        u2[hf, 0, 1] = go(copy(ZS.at[hf, 1, 1], U2.at[hf, 0, 1], to(1)))
        ZS[hf, 2, 0] = add(0, mm)
        u2[hf, 1, 0] = go(copy(ZS.at[hf, 2, 0], U2.at[hf, 1, 0], to(3)))
        for g, mi in ((0, mp), (1, mm), (0, m), (1, m)):
            add(g, mi)
    for hf in range(2):
        m, to = minor[hf], at_minor[hf]
        mp, mm = (m + 1) % 4, (m + 3) % 4
        e2[hf, 0].wait_recv()
        ZS[hf, 1, 0] = (T[hf, 0, mp] + H2[hf, 0].astype(F32)).astype(BF)
        u2[hf, 0, 0] = go(copy(ZS.at[hf, 1, 0], U2.at[hf, 0, 0], to(1)))
        e2[hf, 1].wait_recv()
        ZS[hf, 2, 1] = (T[hf, 1, mm] + H2[hf, 1].astype(F32)).astype(BF)
        u2[hf, 1, 1] = go(copy(ZS.at[hf, 2, 1], U2.at[hf, 1, 1], to(3)))
    for hf in range(2):
        m = minor[hf]
        for dr in range(2):
            for g in range(2):
                u2[hf, dr, g].wait_recv()
        g = 1 - zl
        ZS[hf, 3, 0] = (T[hf, g, m] + U2[hf, 0, g].astype(F32) + U2[hf, 1, g].astype(F32)).astype(BF)
        ez[hf] = go(copy(ZS.at[hf, 3, 0], Z.at[hf], zpart))
    for hf in range(2):
        m = minor[hf]
        rows = slice(hf * 32, hf * 32 + 32)
        own = T[hf, zl, m] + U2[hf, 0, zl].astype(F32) + U2[hf, 1, zl].astype(F32)
        own = own + tok[rows].astype(F32) + bout[...].reshape(1, FEAT)
        ez[hf].wait_recv()
        out[rows] = (own + Z[hf].astype(F32)).astype(BF)

    for d, cond in pending:
        if cond is None:
            d.wait_send()
        else:
            pl.when(cond)(d.wait_send)


SCRATCH = [
    pltpu.VMEM((3, FEAT, UNIT), BF),
    pltpu.VMEM((UNIT, FEAT), BF),
    pltpu.VMEM((64, FEAT), BF),
    pltpu.VMEM((2, 4, 2, 4, 32, FEAT), BF),
    pltpu.VMEM((FEAT, 3 * UNIT), BF),
    pltpu.VMEM((UNIT, FEAT), BF),
    pltpu.VMEM((3, 8, UNIT), F32),
    pltpu.VMEM((10, 8, 128), F32),
    pltpu.VMEM((3, 1024, UNIT), F32),
    pltpu.VMEM((3, 1024, UNIT), BF),
    pltpu.VMEM((3, 1024, UNIT), BF),
    pltpu.VMEM((1024, UNIT), BF),
    pltpu.VMEM((1024, UNIT), BF),
    pltpu.VMEM((2, 1024, UNIT), BF),
    pltpu.VMEM((2, 512, UNIT), BF),
    pltpu.VMEM((2, 512, UNIT), BF),
    pltpu.VMEM((4, 4, 2, 32, HD), BF),
    pltpu.VMEM((2, 4, 2, 4, 2, 32, HD), BF),
    pltpu.VMEM((2, 4, 2, 3, 4, 32, HD), BF),
    pltpu.VMEM((6, 2, 4, 32, FEAT), BF),
    pltpu.VMEM((2, 2, 4, 32, FEAT), BF),
    pltpu.VMEM((2, 2, 2, 4, 32, FEAT), BF),
    pltpu.VMEM((2, 2, 4, 32, FEAT), F32),
    pltpu.VMEM((2, 2, 32, FEAT), BF),
    pltpu.VMEM((2, 2, 2, 32, FEAT), BF),
    pltpu.VMEM((2, 32, FEAT), BF),
    pltpu.VMEM((2, 4, 2, 32, FEAT), BF),
    pltpu.SemaphoreType.DMA((256,)),
    pltpu.SemaphoreType.DMA((256,)),
    pltpu.SemaphoreType.DMA((2,)),
]


def body(tokens, ln_gain, ln_bias, w_qkv, bias_qkv, mask_qkv, w_out, bias_out, mask_out):
    vm = pl.BlockSpec(memory_space=pltpu.VMEM)
    hbm = pl.BlockSpec(memory_space=pl.ANY)
    sm = pl.BlockSpec(memory_space=pltpu.SMEM)
    return pl.pallas_call(
        kernel,
        out_shape=jax.ShapeDtypeStruct((64, FEAT), BF),
        in_specs=[vm, vm, vm, hbm, vm, sm, hbm, vm, sm],
        out_specs=vm,
        scratch_shapes=SCRATCH,
        compiler_params=pltpu.CompilerParams(
            collective_id=0, has_side_effects=True, vmem_limit_bytes=60 * 1024 * 1024),
    )(tokens, ln_gain, ln_bias, w_qkv, bias_qkv, jnp.swapaxes(mask_qkv, 1, 2), w_out, bias_out, mask_out)


def solution(mesh):
    placed = (
        P("col", "row"),
        P("row"),
        P("row"),
        P(None, "row", "col"),
        P(None, "col"),
        P(None, "row", "col"),
        P("col", "row"),
        P("row"),
        P("col", "row"),
    )
    return jax.shard_map(
        body, mesh=mesh, in_specs=placed, out_specs=P("col", "row"), check_vma=False
    )
```

```python
import functools

import jax
import jax.numpy as jnp
from jax import lax
from jax.experimental import pallas as pl
from jax.experimental.pallas import tpu as pltpu
from jax.sharding import PartitionSpec as P

BF, F32 = jnp.bfloat16, jnp.float32
HD = 128
D = 12288
FEAT = 1536
UNIT = 384
HALF, RING = 2, 4

ORDER_IN = (0, 1, 3, 2) + tuple(
    (hf, k0, k1, m, 2) for k0, k1 in ((3, 1), (1, 3), (2, 2)) for m in (0, 2) for hf in (0, 1))
ROWS = 64
OFF = [ROWS * t for t in range(len(ORDER_IN))]
PIECES = len(ORDER_IN)
SCHEDULE = (
    "M0", "N0", "E0", "N1", "M1", "M2", "E1", "L0", "E2", "M3", "E3", "F0", "F1", "P0",
    "K0", "K1", "F2", "H0", "H1", "F3", "W0", "M4", "M5", "E4", "E5", "M6", "M7", "E6",
    "E7", "F4", "F5", "H2", "H3", "K2", "K3", "M8", "M9", "E8", "E9", "F6", "F7", "H4",
    "H5", "K4", "K5", "M10", "M11", "E10", "E11", "F8", "F9", "H6", "H7", "K6", "K7", "G0",
    "G1", "M12", "M13", "E12", "E13", "F10", "F11", "H8", "H9", "K8", "K9", "G2", "G3", "M14",
    "M15", "E14", "E15", "F12", "F13", "H10", "H11", "K10", "K11", "G4", "G5", "G6", "K12", "G7",
    "K13", "F14", "H12", "G8", "K14", "F15", "H13", "G9", "K15", "H14", "G10", "H15", "G11", "G12",
    "G13", "G14", "G15",
)
SCHEDULE_OUT = (
    "S0", "S1", "B0", "S2", "B1", "S3", "C0", "S4", "C1", "S5", "B2", "C2", "B3", "C3", "S6", "S7",
    "B4", "C4", "B5", "C5", "B6", "B7", "D0", "D1", "D2", "D3", "C6", "C7",
)
ORDER_OUT = ((0, 2), (1, 2), (0, 1), (0, 3), (1, 1), (1, 3), (0, 0), (1, 0))


def kernel(tok, gain, lnb, wqkv_hbm, bqkv, mq, wout_hbm, bout, mo, out,
           wqkv, wout, RZ, X, W, WO, BH, stat, S, SB, SR, SUP, SDN, UR, HS, HR, Q, KV, C,
           PO, H1, U1, T, H2, U2, Z, ZS, ssem, rsem, lsem):
    r, c = lax.axis_index("row"), lax.axis_index("col")
    core, h = r % 2, r // 2
    y, zl, x = c % 4, (c // 4) % 2, c // 8
    sib = (r + 1 - 2 * core, c)
    hup, hdn, hop = ((r + 2) % 8, c), ((r + 6) % 8, c), ((r + 4) % 8, c)
    zpart = (r, c + 4 - 8 * zl)

    def at_x(k):
        return (r, ((x + k) % 4) * 8 + zl * 4 + y)

    def at_y(k):
        return (r, x * 8 + zl * 4 + (y + k) % 4)

    lead, minor = (x, y), (y, x)
    at_lead, at_minor = (at_x, at_y), (at_y, at_x)
    p = (h + 1 + 2 * zl) % 4

    ids = [0]
    pending = []

    def copy(src, dst, to):
        i = ids[0]
        ids[0] += 1
        return pltpu.make_async_remote_copy(
            src_ref=src, dst_ref=dst, send_sem=ssem.at[i], recv_sem=rsem.at[i],
            device_id=to, device_id_type=pl.DeviceIdType.MESH)

    def go(d, cond=None):
        pending.append((d, cond))
        d.start()
        return d

    load_w = pltpu.make_async_copy(wqkv_hbm, wqkv, lsem.at[0])
    load_w.start()
    load_o = pltpu.make_async_copy(wout_hbm, wout, lsem.at[1])
    load_o.start()
    peers = [((r + k) % 8, c) for k in range(1, 8)]
    partners = peers + [zpart, at_x(1), at_x(3), at_y(1), at_y(3)]
    bar = pltpu.get_barrier_semaphore()
    for d in partners:
        pl.semaphore_signal(bar, inc=1, device_id=d, device_id_type=pl.DeviceIdType.MESH)

    def prune_qkv(part):
        for i in part:
            rows = slice(i * HD, i * HD + HD)
            for a in range(3):
                for k in range(3):
                    w = wqkv[k, rows, a * HD:a * HD + HD].astype(F32) * mq[k, a, i].astype(F32)
                    W[rows, a * UNIT + k * HD:a * UNIT + k * HD + HD] = w.astype(BF)

    vals = tok[...].astype(F32)
    s1 = jnp.sum(vals, axis=1, keepdims=True)
    s2 = jnp.sum(vals * vals, axis=1, keepdims=True)
    lane = lax.broadcasted_iota(jnp.int32, (64, 128), 1)
    line = lax.broadcasted_iota(jnp.int32, (64, 128), 0)
    packed = jnp.where(lane == line, s1, 0.0) + jnp.where(lane == line + 64, s2, 0.0)
    stat[0] = jnp.broadcast_to(jnp.sum(packed, axis=0, keepdims=True), (8, 128))
    pl.semaphore_wait(bar, len(partners))
    ds = [go(copy(stat.at[0], stat.at[k + 1], to)) for k, to in enumerate(peers)]
    raw = go(copy(tok, RZ, zpart))
    load_w.wait()
    prune_qkv(range(0, 6))
    for a in range(3):
        BH[a] = jnp.broadcast_to(
            jnp.concatenate([bqkv[k:k + 1, a * HD:a * HD + HD] for k in range(3)], axis=1), (8, UNIT))
    tot = stat[0]
    for k, d in enumerate(ds):
        d.wait_recv()
        tot = tot + stat[k + 1]
    stat[8] = tot
    dt = go(copy(stat.at[8], stat.at[9], zpart))

    def normalise(values, sums, gz):
        sums = sums[0:1]
        mean = jnp.sum(jnp.where(lane == line, sums, 0.0), axis=1, keepdims=True) * (1.0 / D)
        square = jnp.sum(jnp.where(lane == line + 64, sums, 0.0), axis=1, keepdims=True) * (1.0 / D)
        var = square - mean * mean
        normed = (values - mean) * lax.rsqrt(var + 1e-5) * gain[...].reshape(1, FEAT) + lnb[...].reshape(1, FEAT)
        normed = normed.astype(BF)
        for hf in range(2):
            X[hf, lead[hf], gz, minor[hf]] = normed[hf * 32:hf * 32 + 32]

    d1 = {}

    def send_minor(g):
        for hf in range(2):
            ref = X.at[hf, lead[hf], zl if g == 0 else 1 - zl, minor[hf]]
            for k in (1, 3):
                d1[hf, g, k] = go(copy(ref, ref, at_minor[hf](k)))

    normalise(vals, tot, zl)
    send_minor(0)
    prune_qkv(range(6, 12))
    raw.wait_recv()
    dt.wait_recv()
    normalise(RZ[...].astype(F32), stat[9], 1 - zl)
    send_minor(1)

    df, d2 = {}, {}

    def pass_minor(g):
        gz = zl if g == 0 else 1 - zl
        step = 1 + 2 * gz
        for hf in range(2):
            for k in (1, 3):
                d1[hf, g, k].wait_recv()
            ref = X.at[hf, lead[hf], gz, (minor[hf] + 4 - step) % 4]
            df[hf, g] = go(copy(ref, ref, at_minor[hf](step)))

    def send_lead(_):
        for hf in range(2):
            for g in range(2):
                df[hf, g].wait_recv()
        for g in range(2):
            for hf in range(2):
                for k, gg in ((1, g), (3, 1 - g)):
                    ref = X.at[hf, lead[hf], gg]
                    d2[hf, k, gg] = go(copy(ref, ref, at_lead[hf](k)))

    def forward_lead(hf):
        for k, gg in ((1, 0), (3, 1)):
            d2[hf, k, gg].wait_recv()
            ref = X.at[hf, (lead[hf] + 4 - k) % 4, gg]
            d2[hf, 2, gg] = go(copy(ref, ref, at_lead[hf](k)))

    dsib, dup, ddn, dhup, dhdn, dkv = {}, {}, {}, {}, {}, {}

    waited = {(h_, k_, g_) for h_ in range(2) for k_, g_ in ((1, 0), (3, 1))}

    def span(t):
        n = ROWS
        return n, slice(OFF[t], OFF[t] + n), pl.ds(OFF[t], n), pl.ds(OFF[t] // 2, n // 2)

    def stage_m(t):
        n, at, ds_, _ = span(t)
        if t < 4:
            k = ORDER_IN[t]
            rows = jnp.concatenate(
                [X[hf, lead[hf], z, (minor[hf] + k) % 4] for z in (core, 1 - core) for hf in range(2)], axis=0)
        else:
            hf, k0, k1, m0, mn = ORDER_IN[t]
            for k, gg in ((k0, 0), (k1, 1)):
                if (hf, 4 - k, gg) not in waited:
                    d2[hf, 4 - k, gg].wait_recv()
                    waited.add((hf, 4 - k, gg))
            l = [(lead[hf] + k) % 4 for k in (k0, k1)]
            own, other = jnp.where(core == 0, l[0], l[1]), jnp.where(core == 0, l[1], l[0])
            rows = jnp.concatenate(
                [X[hf, own, core, m0:m0 + mn].reshape(n, FEAT),
                 X[hf, other, 1 - core, m0:m0 + mn].reshape(n, FEAT)], axis=0)
        acc = jnp.dot(rows, W[...], preferred_element_type=F32)
        for a in range(3):
            S[a, at] = acc[:n, a * UNIT:a * UNIT + UNIT]
            SB[a, at] = acc[n:, a * UNIT:a * UNIT + UNIT].astype(BF)
        dsib[t] = go(copy(SB.at[:, ds_], SR.at[:, ds_], sib))

    def stage_e(t):
        n, at, ds_, hs_ = span(t)
        mid, low = OFF[t] + n // 2, slice(OFF[t] // 2, OFF[t] // 2 + n // 2)
        dsib[t].wait_recv()
        for a in range(3):
            S[a, at] = S[a, at] + SR[a, at].astype(F32)
        dup[t] = copy(SUP.at[ds_], UR.at[0, ds_], hup)
        ddn[t] = copy(SDN.at[ds_], UR.at[1, ds_], hdn)
        dhup[t] = copy(HS.at[0, hs_], HR.at[0, hs_], hup)
        dhdn[t] = copy(HS.at[1, hs_], HR.at[1, hs_], hdn)
        pending.extend([(dup[t], None), (ddn[t], None), (dhup[t], p == 0), (dhdn[t], p == 0)])

        @pl.when(p == 3)
        def _():
            SUP[at] = S[0, at].astype(BF)
            dup[t].start()

        @pl.when(p == 1)
        def _():
            SDN[at] = S[2, at].astype(BF)
            ddn[t].start()

        @pl.when(p == 0)
        def _():
            HS[0, low] = S[1, OFF[t]:mid].astype(BF)
            dhup[t].start()
            HS[1, low] = S[1, mid:OFF[t] + n].astype(BF)
            dhdn[t].start()

    def stage_k(t):
        _, at, _, _ = span(t)

        @pl.when(p == 2)
        def _():
            SUP[at] = S[2, at].astype(BF)
            dup[t].start()
            SDN[at] = S[0, at].astype(BF)
            ddn[t].start()

    def stage_f(t):
        _, at, _, _ = span(t)

        @pl.when(p == 0)
        def _():
            dup[t].wait_recv()
            SUP[at] = (S[0, at] + UR[0, at].astype(F32)).astype(BF)
            dup[t].start()
            ddn[t].wait_recv()
            SDN[at] = (S[2, at] + UR[1, at].astype(F32)).astype(BF)
            ddn[t].start()

    def stage_h(t):
        n, at, _, _ = span(t)
        mid, low = OFF[t] + n // 2, slice(OFF[t] // 2, OFF[t] // 2 + n // 2)
        first, second = slice(OFF[t], mid), slice(mid, OFF[t] + n)

        @pl.when(p == 1)
        def _():
            SUP[second] = S[1, second].astype(BF)
            dhup[t].wait_recv()
            SUP[first] = (S[1, first] + HR[0, low].astype(F32)).astype(BF)
            dup[t].start()

        @pl.when(p == 3)
        def _():
            SDN[first] = S[1, first].astype(BF)
            dhdn[t].wait_recv()
            SDN[second] = (S[1, second] + HR[1, low].astype(F32)).astype(BF)
            ddn[t].start()

    def stage_g(t):
        _, at, _, _ = span(t)
        if t < 4:
            k = ORDER_IN[t]
            blocks = ((x, (y + k) % 4, 0), ((x + k) % 4, y, 1))
            refs = [KV.at[:, bx, core, by, hf] for bx, by, hf in blocks]
        else:
            hf, k0, k1, m0, mn = ORDER_IN[t]
            l = (lead[hf] + jnp.where(core == 0, k0, k1)) % 4
            ms = pl.ds(m0, mn)
            refs = [KV.at[:, l, core, ms, 0] if hf == 0 else KV.at[:, ms, core, l, 1]]
            blocks = [(l, m0 + m, 0) if hf == 0 else (m0 + m, l, 1) for m in range(mn)]
        dkv[t] = [copy(ref, ref, sib) for ref in refs]
        pending.extend([(d, p > 0) for d in dkv[t]])

        @pl.when(p > 0)
        def _():
            dup[t].wait_recv()
            ddn[t].wait_recv()
            total = S[p - 1, at] + UR[0, at].astype(F32) + UR[1, at].astype(F32) + BH[p - 1][0:1]
            total = total.astype(BF)
            for m, (bx, by, hf) in enumerate(blocks):
                part = total[m * 32:m * 32 + 32]
                Q[bx, by, hf] = part[:, 0:HD]
                KV[0, bx, core, by, hf] = part[:, HD:2 * HD]
                KV[1, bx, core, by, hf] = part[:, 2 * HD:]
            for d in dkv[t]:
                d.start()

    def prune_out():
        load_o.wait()
        for i in range(3):
            for j in range(12):
                blk = (slice(i * HD, i * HD + HD), slice(j * HD, j * HD + HD))
                WO[blk] = (wout[blk].astype(F32) * mo[i, j].astype(F32)).astype(BF)

    def pass_on(t):
        forward_lead(0)
        forward_lead(1)

    stages = dict(N=pass_minor, L=send_lead, M=stage_m, E=stage_e, F=stage_f, H=stage_h, K=stage_k, G=stage_g, W=pass_on, P=lambda t: prune_out())
    for word in SCHEDULE:
        stages[word[0]](int(word[1:]))

    a_own = jnp.where(p > 0, p - 1, 0)

    @pl.when(p > 0)
    def _():
        for t in range(PIECES):
            for d in dkv[t]:
                d.wait_recv()
        scale = 1.4426950408889634 / (HD ** 0.5)
        for b in range(4):
            n = 512 * (b + 1)
            q = Q[b].reshape(256, HD)
            keys = KV[0, 0:b + 1].reshape(n, HD)
            values = KV[1, 0:b + 1].reshape(n, HD)
            s = lax.dot_general(q, keys, (((1,), (1,)), ((), ())), preferred_element_type=F32)
            qpos = lax.broadcasted_iota(jnp.int32, (256, 512), 0) + core * 256
            kpos = lax.broadcasted_iota(jnp.int32, (256, 512), 1)
            diag = jnp.where(kpos <= qpos, s[:, n - 512:], -jnp.inf)
            s = diag if b == 0 else jnp.concatenate([s[:, :n - 512], diag], axis=1)
            top = jnp.max(s, axis=1, keepdims=True)
            e = jnp.exp2((s - top) * scale)
            inv = 1.0 / jnp.sum(e, axis=1, keepdims=True)
            ctx = jnp.dot((e * inv).astype(BF), values, preferred_element_type=F32).astype(BF)
            ctx = ctx.reshape(4, 2, 32, HD)
            for m in range(4):
                C[0, b, core, a_own, m] = ctx[m, 0]
                C[1, m, core, a_own, b] = ctx[m, 1]

    dctx, cs = {}, {}

    def send_ctx(t):
        hf, k = ORDER_OUT[t]
        ref = C.at[hf, (lead[hf] + k) % 4, core, a_own]
        dctx[t] = [copy(ref, ref, to) for to in (hup, hdn, hop)]
        pending.extend([(d, p > 0) for d in dctx[t]])

        @pl.when(p > 0)
        def _():
            for d in dctx[t]:
                d.start()

    def stage_b(t):
        hf, k = ORDER_OUT[t]
        for d, cond in zip(dctx[t], (p != 1, p != 3, p != 2)):
            pl.when(cond)(d.wait_recv)
        ref = C.at[hf, (lead[hf] + k) % 4, core]
        cs[t] = go(copy(ref, ref, sib))

    e1, u1 = {}, {}

    def stage_c(t):
        hf, k = ORDER_OUT[t]
        l = (lead[hf] + k) % 4
        cs[t].wait_recv()
        rows = jnp.concatenate(
            [jnp.concatenate([C[hf, l, g, a].reshape(128, HD) for a in range(3)], axis=1)
             for g in range(2)], axis=0)
        acc = jnp.dot(rows, WO[...], preferred_element_type=F32)
        lo, hi = acc[:128].reshape(4, 32, FEAT), acc[128:].reshape(4, 32, FEAT)
        if k == 2:
            PO[t, 0] = lo.astype(BF)
            e1[hf, 0] = go(copy(PO.at[t, 0], H1.at[hf, 0], at_lead[hf](1)))
            PO[t, 1] = hi.astype(BF)
            e1[hf, 1] = go(copy(PO.at[t, 1], H1.at[hf, 1], at_lead[hf](3)))
        elif k == 1:
            PO[t, 1] = hi.astype(BF)
            u1[hf, 0, 1] = go(copy(PO.at[t, 1], U1.at[hf, 0, 1], at_lead[hf](1)))
            PO[t, 0] = lo.astype(BF)
        elif k == 3:
            PO[t, 0] = lo.astype(BF)
            u1[hf, 1, 0] = go(copy(PO.at[t, 0], U1.at[hf, 1, 0], at_lead[hf](3)))
            PO[t, 1] = hi.astype(BF)
        else:
            T[hf, 0] = lo
            T[hf, 1] = hi

    def stage_d(hf, g):
        k = 1 if g == 0 else 3
        t = ORDER_OUT.index((hf, k))
        e1[hf, g].wait_recv()
        for step in (2, 1, 3, 0):
            mi = (minor[hf] + step) % 4
            PO[t, g, mi] = (PO[t, g, mi].astype(F32) + H1[hf, g, mi].astype(F32)).astype(BF)
            u1[hf, g, g, step] = go(copy(PO.at[t, g, mi], U1.at[hf, g, g, mi], at_lead[hf](k)))

    stages = dict(S=send_ctx, B=stage_b, C=stage_c, D=lambda i: stage_d(i // 2, i % 2))
    for word in SCHEDULE_OUT:
        stages[word[0]](int(word[1:]))

    e2, u2, ez = {}, {}, {}

    def add(hf, g, step):
        mi = (minor[hf] + step) % 4
        u1[hf, g, g, step].wait_recv()
        t_ = T[hf, g, mi] + U1[hf, 0, g, mi].astype(F32) + U1[hf, 1, g, mi].astype(F32)
        T[hf, g, mi] = t_
        return t_.astype(BF)

    for hf in range(2):
        to = at_minor[hf]
        u1[hf, 0, 1].wait_recv()
        u1[hf, 1, 0].wait_recv()
        for g in range(2):
            ZS[hf, 0, g] = add(hf, g, 2)
            e2[hf, g] = go(copy(ZS.at[hf, 0, g], H2.at[hf, g], to(1 + 2 * g)))
    for hf in range(2):
        to = at_minor[hf]
        ZS[hf, 1, 1] = add(hf, 1, 1)
        u2[hf, 0, 1] = go(copy(ZS.at[hf, 1, 1], U2.at[hf, 0, 1], to(1)))
        ZS[hf, 2, 0] = add(hf, 0, 3)
        u2[hf, 1, 0] = go(copy(ZS.at[hf, 2, 0], U2.at[hf, 1, 0], to(3)))
    for hf in range(2):
        for g, step in ((0, 1), (1, 3), (0, 0), (1, 0)):
            add(hf, g, step)
    for hf in range(2):
        m, to = minor[hf], at_minor[hf]
        mp, mm = (m + 1) % 4, (m + 3) % 4
        e2[hf, 0].wait_recv()
        ZS[hf, 1, 0] = (T[hf, 0, mp] + H2[hf, 0].astype(F32)).astype(BF)
        u2[hf, 0, 0] = go(copy(ZS.at[hf, 1, 0], U2.at[hf, 0, 0], to(1)))
        e2[hf, 1].wait_recv()
        ZS[hf, 2, 1] = (T[hf, 1, mm] + H2[hf, 1].astype(F32)).astype(BF)
        u2[hf, 1, 1] = go(copy(ZS.at[hf, 2, 1], U2.at[hf, 1, 1], to(3)))
    for hf in range(2):
        m = minor[hf]
        for dr in range(2):
            for g in range(2):
                u2[hf, dr, g].wait_recv()
        g = 1 - zl
        ZS[hf, 3, 0] = (T[hf, g, m] + U2[hf, 0, g].astype(F32) + U2[hf, 1, g].astype(F32)).astype(BF)
        ez[hf] = go(copy(ZS.at[hf, 3, 0], Z.at[hf], zpart))
    for hf in range(2):
        m = minor[hf]
        rows = slice(hf * 32, hf * 32 + 32)
        own = T[hf, zl, m] + U2[hf, 0, zl].astype(F32) + U2[hf, 1, zl].astype(F32)
        own = own + tok[rows].astype(F32) + bout[...].reshape(1, FEAT)
        ez[hf].wait_recv()
        out[rows] = (own + Z[hf].astype(F32)).astype(BF)

    for d, cond in pending:
        if cond is None:
            d.wait_send()
        else:
            pl.when(cond)(d.wait_send)


SCRATCH = [
    pltpu.VMEM((3, FEAT, UNIT), BF),
    pltpu.VMEM((UNIT, FEAT), BF),
    pltpu.VMEM((64, FEAT), BF),
    pltpu.VMEM((2, 4, 2, 4, 32, FEAT), BF),
    pltpu.VMEM((FEAT, 3 * UNIT), BF),
    pltpu.VMEM((UNIT, FEAT), BF),
    pltpu.VMEM((3, 8, UNIT), F32),
    pltpu.VMEM((10, 8, 128), F32),
    pltpu.VMEM((3, 1024, UNIT), F32),
    pltpu.VMEM((3, 1024, UNIT), BF),
    pltpu.VMEM((3, 1024, UNIT), BF),
    pltpu.VMEM((1024, UNIT), BF),
    pltpu.VMEM((1024, UNIT), BF),
    pltpu.VMEM((2, 1024, UNIT), BF),
    pltpu.VMEM((2, 512, UNIT), BF),
    pltpu.VMEM((2, 512, UNIT), BF),
    pltpu.VMEM((4, 4, 2, 32, HD), BF),
    pltpu.VMEM((2, 4, 2, 4, 2, 32, HD), BF),
    pltpu.VMEM((2, 4, 2, 3, 4, 32, HD), BF),
    pltpu.VMEM((6, 2, 4, 32, FEAT), BF),
    pltpu.VMEM((2, 2, 4, 32, FEAT), BF),
    pltpu.VMEM((2, 2, 2, 4, 32, FEAT), BF),
    pltpu.VMEM((2, 2, 4, 32, FEAT), F32),
    pltpu.VMEM((2, 2, 32, FEAT), BF),
    pltpu.VMEM((2, 2, 2, 32, FEAT), BF),
    pltpu.VMEM((2, 32, FEAT), BF),
    pltpu.VMEM((2, 4, 2, 32, FEAT), BF),
    pltpu.SemaphoreType.DMA((256,)),
    pltpu.SemaphoreType.DMA((256,)),
    pltpu.SemaphoreType.DMA((2,)),
]


def body(tokens, ln_gain, ln_bias, w_qkv, bias_qkv, mask_qkv, w_out, bias_out, mask_out):
    vm = pl.BlockSpec(memory_space=pltpu.VMEM)
    hbm = pl.BlockSpec(memory_space=pl.ANY)
    sm = pl.BlockSpec(memory_space=pltpu.SMEM)
    return pl.pallas_call(
        kernel,
        out_shape=jax.ShapeDtypeStruct((64, FEAT), BF),
        in_specs=[vm, vm, vm, hbm, vm, sm, hbm, vm, sm],
        out_specs=vm,
        scratch_shapes=SCRATCH,
        compiler_params=pltpu.CompilerParams(
            collective_id=0, has_side_effects=True, vmem_limit_bytes=60 * 1024 * 1024),
    )(tokens, ln_gain, ln_bias, w_qkv, bias_qkv, jnp.swapaxes(mask_qkv, 1, 2), w_out, bias_out, mask_out)


def solution(mesh):
    placed = (
        P("col", "row"),
        P("row"),
        P("row"),
        P(None, "row", "col"),
        P(None, "col"),
        P(None, "row", "col"),
        P("col", "row"),
        P("row"),
        P("col", "row"),
    )
    return jax.shard_map(
        body, mesh=mesh, in_specs=placed, out_specs=P("col", "row"), check_vma=False
    )
```

```python
import functools

import jax
import jax.numpy as jnp
from jax import lax
from jax.experimental import pallas as pl
from jax.experimental.pallas import tpu as pltpu
from jax.sharding import PartitionSpec as P

BF, F32 = jnp.bfloat16, jnp.float32
HD = 128
D = 12288
FEAT = 1536
UNIT = 384
HALF, RING = 2, 4

ORDER_IN = (0, 1, 3, 2) + tuple(
    (hf, k0, k1, m, 2) for k0, k1 in ((3, 1), (1, 3), (2, 2)) for m in (0, 2) for hf in (0, 1))
ROWS = 64
OFF = [ROWS * t for t in range(len(ORDER_IN))]
PIECES = len(ORDER_IN)
SCHEDULE = (
    "M0", "N0", "E0", "N1", "M1", "M2", "E1", "L0", "E2", "M3", "E3", "F0", "F1", "P0",
    "K0", "K1", "F2", "H0", "H1", "F3", "W0", "M4", "M5", "E4", "E5", "M6", "M7", "E6",
    "E7", "F4", "F5", "H2", "H3", "K2", "K3", "M8", "M9", "E8", "E9", "F6", "F7", "H4",
    "H5", "K4", "K5", "M10", "M11", "E10", "E11", "F8", "F9", "H6", "H7", "K6", "K7", "G0",
    "G1", "M12", "M13", "E12", "E13", "F10", "F11", "H8", "H9", "K8", "K9", "G2", "G3", "M14",
    "M15", "E14", "E15", "F12", "F13", "H10", "H11", "K10", "K11", "G4", "G5", "G6", "K12", "G7",
    "K13", "F14", "H12", "G8", "K14", "F15", "H13", "G9", "K15", "H14", "G10", "H15", "G11", "G12",
    "G13", "G14", "G15",
)
SCHEDULE_OUT = (
    "S0", "S1", "B0", "S2", "B1", "S3", "C0", "S4", "C1", "S5", "B2", "C2", "B3", "C3", "S6", "S7",
    "B4", "C4", "B5", "C5", "B6", "B7", "D0", "D1", "D2", "D3", "C6", "C7",
)
ORDER_OUT = ((0, 2), (1, 2), (0, 1), (0, 3), (1, 1), (1, 3), (0, 0), (1, 0))


def kernel(tok, gain, lnb, wqkv_hbm, bqkv, mq, wout_hbm, bout, mo, out,
           wqkv, wout, RZ, X, W, WO, BH, stat, S, SB, SR, SUP, SDN, UR, HS, HR, Q, KV, C,
           PO, H1, U1, T, H2, U2, Z, ZS, ssem, rsem, lsem):
    r, c = lax.axis_index("row"), lax.axis_index("col")
    core, h = r % 2, r // 2
    y, zl, x = c % 4, (c // 4) % 2, c // 8
    sib = (r + 1 - 2 * core, c)
    hup, hdn, hop = ((r + 2) % 8, c), ((r + 6) % 8, c), ((r + 4) % 8, c)
    zpart = (r, c + 4 - 8 * zl)

    def at_x(k):
        return (r, ((x + k) % 4) * 8 + zl * 4 + y)

    def at_y(k):
        return (r, x * 8 + zl * 4 + (y + k) % 4)

    lead, minor = (x, y), (y, x)
    at_lead, at_minor = (at_x, at_y), (at_y, at_x)
    p = (h + 1 + 2 * zl) % 4

    ids = [0]
    pending = []

    def copy(src, dst, to):
        i = ids[0]
        ids[0] += 1
        return pltpu.make_async_remote_copy(
            src_ref=src, dst_ref=dst, send_sem=ssem.at[i], recv_sem=rsem.at[i],
            device_id=to, device_id_type=pl.DeviceIdType.MESH)

    def go(d, cond=None):
        pending.append((d, cond))
        d.start()
        return d

    load_w = pltpu.make_async_copy(wqkv_hbm, wqkv, lsem.at[0])
    load_w.start()
    load_o = pltpu.make_async_copy(wout_hbm, wout, lsem.at[1])
    load_o.start()
    peers = [((r + k) % 8, c) for k in range(1, 8)]
    partners = peers + [zpart, at_x(1), at_x(3), at_y(1), at_y(3)]
    bar = pltpu.get_barrier_semaphore()
    for d in partners:
        pl.semaphore_signal(bar, inc=1, device_id=d, device_id_type=pl.DeviceIdType.MESH)

    def prune_qkv(part):
        for i in part:
            rows = slice(i * HD, i * HD + HD)
            for a in range(3):
                for k in range(3):
                    w = wqkv[k, rows, a * HD:a * HD + HD].astype(F32) * mq[k, a, i].astype(F32)
                    W[rows, a * UNIT + k * HD:a * UNIT + k * HD + HD] = w.astype(BF)

    vals = tok[...].astype(F32)
    s1 = jnp.sum(vals, axis=1, keepdims=True)
    s2 = jnp.sum(vals * vals, axis=1, keepdims=True)
    lane = lax.broadcasted_iota(jnp.int32, (64, 128), 1)
    line = lax.broadcasted_iota(jnp.int32, (64, 128), 0)
    packed = jnp.where(lane == line, s1, 0.0) + jnp.where(lane == line + 64, s2, 0.0)
    stat[0] = jnp.broadcast_to(jnp.sum(packed, axis=0, keepdims=True), (8, 128))
    pl.semaphore_wait(bar, len(partners))
    ds = [go(copy(stat.at[0], stat.at[k + 1], to)) for k, to in enumerate(peers)]
    raw = go(copy(tok, RZ, zpart))
    load_w.wait()
    prune_qkv(range(0, 6))
    for a in range(3):
        BH[a] = jnp.broadcast_to(
            jnp.concatenate([bqkv[k:k + 1, a * HD:a * HD + HD] for k in range(3)], axis=1), (8, UNIT))
    tot = stat[0]
    for k, d in enumerate(ds):
        d.wait_recv()
        tot = tot + stat[k + 1]
    stat[8] = tot
    dt = go(copy(stat.at[8], stat.at[9], zpart))

    def normalise(values, sums, gz):
        sums = sums[0:1]
        mean = jnp.sum(jnp.where(lane == line, sums, 0.0), axis=1, keepdims=True) * (1.0 / D)
        square = jnp.sum(jnp.where(lane == line + 64, sums, 0.0), axis=1, keepdims=True) * (1.0 / D)
        var = square - mean * mean
        normed = (values - mean) * lax.rsqrt(var + 1e-5) * gain[...].reshape(1, FEAT) + lnb[...].reshape(1, FEAT)
        normed = normed.astype(BF)
        for hf in range(2):
            X[hf, lead[hf], gz, minor[hf]] = normed[hf * 32:hf * 32 + 32]

    d1 = {}

    def send_minor(g):
        for hf in range(2):
            ref = X.at[hf, lead[hf], zl if g == 0 else 1 - zl, minor[hf]]
            for k in (1, 3):
                d1[hf, g, k] = go(copy(ref, ref, at_minor[hf](k)))

    normalise(vals, tot, zl)
    send_minor(0)
    prune_qkv(range(6, 12))
    raw.wait_recv()
    dt.wait_recv()
    normalise(RZ[...].astype(F32), stat[9], 1 - zl)
    send_minor(1)

    df, d2 = {}, {}

    def pass_minor(g):
        gz = zl if g == 0 else 1 - zl
        step = 1 + 2 * gz
        for hf in range(2):
            for k in (1, 3):
                d1[hf, g, k].wait_recv()
            ref = X.at[hf, lead[hf], gz, (minor[hf] + 4 - step) % 4]
            df[hf, g] = go(copy(ref, ref, at_minor[hf](step)))

    def send_lead(_):
        for hf in range(2):
            for g in range(2):
                df[hf, g].wait_recv()
        for g in range(2):
            for hf in range(2):
                for k, gg in ((1, g), (3, 1 - g)):
                    ref = X.at[hf, lead[hf], gg]
                    d2[hf, k, gg] = go(copy(ref, ref, at_lead[hf](k)))

    def forward_lead(hf):
        for k, gg in ((1, 0), (3, 1)):
            d2[hf, k, gg].wait_recv()
            ref = X.at[hf, (lead[hf] + 4 - k) % 4, gg]
            d2[hf, 2, gg] = go(copy(ref, ref, at_lead[hf](k)))

    dsib, dup, ddn, dhup, dhdn, dkv = {}, {}, {}, {}, {}, {}

    waited = {(h_, k_, g_) for h_ in range(2) for k_, g_ in ((1, 0), (3, 1))}

    def span(t):
        n = ROWS
        return n, slice(OFF[t], OFF[t] + n), pl.ds(OFF[t], n), pl.ds(OFF[t] // 2, n // 2)

    def stage_m(t):
        n, at, ds_, _ = span(t)
        if t < 4:
            k = ORDER_IN[t]
            rows = jnp.concatenate(
                [X[hf, lead[hf], z, (minor[hf] + k) % 4] for z in (core, 1 - core) for hf in range(2)], axis=0)
        else:
            hf, k0, k1, m0, mn = ORDER_IN[t]
            for k, gg in ((k0, 0), (k1, 1)):
                if (hf, 4 - k, gg) not in waited:
                    d2[hf, 4 - k, gg].wait_recv()
                    waited.add((hf, 4 - k, gg))
            l = [(lead[hf] + k) % 4 for k in (k0, k1)]
            own, other = jnp.where(core == 0, l[0], l[1]), jnp.where(core == 0, l[1], l[0])
            rows = jnp.concatenate(
                [X[hf, own, core, m0:m0 + mn].reshape(n, FEAT),
                 X[hf, other, 1 - core, m0:m0 + mn].reshape(n, FEAT)], axis=0)
        acc = jnp.dot(rows, W[...], preferred_element_type=F32)
        for a in range(3):
            S[a, at] = acc[:n, a * UNIT:a * UNIT + UNIT]
            SB[a, at] = acc[n:, a * UNIT:a * UNIT + UNIT].astype(BF)
        dsib[t] = go(copy(SB.at[:, ds_], SR.at[:, ds_], sib))

    def stage_e(t):
        n, at, ds_, hs_ = span(t)
        mid, low = OFF[t] + n // 2, slice(OFF[t] // 2, OFF[t] // 2 + n // 2)
        dsib[t].wait_recv()
        for a in range(3):
            S[a, at] = S[a, at] + SR[a, at].astype(F32)
        dup[t] = copy(SUP.at[ds_], UR.at[0, ds_], hup)
        ddn[t] = copy(SDN.at[ds_], UR.at[1, ds_], hdn)
        dhup[t] = copy(HS.at[0, hs_], HR.at[0, hs_], hup)
        dhdn[t] = copy(HS.at[1, hs_], HR.at[1, hs_], hdn)
        pending.extend([(dup[t], None), (ddn[t], None), (dhup[t], p == 0), (dhdn[t], p == 0)])

        @pl.when(p == 3)
        def _():
            SUP[at] = S[0, at].astype(BF)
            dup[t].start()

        @pl.when(p == 1)
        def _():
            SDN[at] = S[2, at].astype(BF)
            ddn[t].start()

        @pl.when(p == 0)
        def _():
            HS[0, low] = S[1, OFF[t]:mid].astype(BF)
            dhup[t].start()
            HS[1, low] = S[1, mid:OFF[t] + n].astype(BF)
            dhdn[t].start()

    def stage_k(t):
        _, at, _, _ = span(t)

        @pl.when(p == 2)
        def _():
            SUP[at] = S[2, at].astype(BF)
            dup[t].start()
            SDN[at] = S[0, at].astype(BF)
            ddn[t].start()

    def stage_f(t):
        _, at, _, _ = span(t)

        @pl.when(p == 0)
        def _():
            dup[t].wait_recv()
            SUP[at] = (S[0, at] + UR[0, at].astype(F32)).astype(BF)
            dup[t].start()
            ddn[t].wait_recv()
            SDN[at] = (S[2, at] + UR[1, at].astype(F32)).astype(BF)
            ddn[t].start()

    def stage_h(t):
        n, at, _, _ = span(t)
        mid, low = OFF[t] + n // 2, slice(OFF[t] // 2, OFF[t] // 2 + n // 2)
        first, second = slice(OFF[t], mid), slice(mid, OFF[t] + n)

        @pl.when(p == 1)
        def _():
            SUP[second] = S[1, second].astype(BF)
            dhup[t].wait_recv()
            SUP[first] = (S[1, first] + HR[0, low].astype(F32)).astype(BF)
            dup[t].start()

        @pl.when(p == 3)
        def _():
            SDN[first] = S[1, first].astype(BF)
            dhdn[t].wait_recv()
            SDN[second] = (S[1, second] + HR[1, low].astype(F32)).astype(BF)
            ddn[t].start()

    def stage_g(t):
        _, at, _, _ = span(t)
        if t < 4:
            k = ORDER_IN[t]
            blocks = ((x, (y + k) % 4, 0), ((x + k) % 4, y, 1))
            refs = [KV.at[:, bx, core, by, hf] for bx, by, hf in blocks]
        else:
            hf, k0, k1, m0, mn = ORDER_IN[t]
            l = (lead[hf] + jnp.where(core == 0, k0, k1)) % 4
            ms = pl.ds(m0, mn)
            refs = [KV.at[:, l, core, ms, 0] if hf == 0 else KV.at[:, ms, core, l, 1]]
            blocks = [(l, m0 + m, 0) if hf == 0 else (m0 + m, l, 1) for m in range(mn)]
        dkv[t] = [copy(ref, ref, sib) for ref in refs]
        pending.extend([(d, p > 0) for d in dkv[t]])

        @pl.when(p > 0)
        def _():
            dup[t].wait_recv()
            ddn[t].wait_recv()
            total = S[p - 1, at] + UR[0, at].astype(F32) + UR[1, at].astype(F32) + BH[p - 1][0:1]
            total = total.astype(BF)
            for m, (bx, by, hf) in enumerate(blocks):
                part = total[m * 32:m * 32 + 32]
                Q[bx, by, hf] = part[:, 0:HD]
                KV[0, bx, core, by, hf] = part[:, HD:2 * HD]
                KV[1, bx, core, by, hf] = part[:, 2 * HD:]
            for d in dkv[t]:
                d.start()

    def prune_out():
        load_o.wait()
        for i in range(3):
            for j in range(12):
                blk = (slice(i * HD, i * HD + HD), slice(j * HD, j * HD + HD))
                WO[blk] = (wout[blk].astype(F32) * mo[i, j].astype(F32)).astype(BF)

    def pass_on(t):
        forward_lead(0)
        forward_lead(1)

    stages = dict(N=pass_minor, L=send_lead, M=stage_m, E=stage_e, F=stage_f, H=stage_h, K=stage_k, G=stage_g, W=pass_on, P=lambda t: prune_out())
    for word in SCHEDULE:
        stages[word[0]](int(word[1:]))

    a_own = jnp.where(p > 0, p - 1, 0)

    @pl.when(p > 0)
    def _():
        for t in range(PIECES):
            for d in dkv[t]:
                d.wait_recv()
        scale = 1.4426950408889634 / (HD ** 0.5)
        for b in range(4):
            n = 512 * (b + 1)
            q = Q[b].reshape(256, HD)
            keys = KV[0, 0:b + 1].reshape(n, HD)
            values = KV[1, 0:b + 1].reshape(n, HD)
            s = lax.dot_general(q, keys, (((1,), (1,)), ((), ())), preferred_element_type=F32)
            qpos = lax.broadcasted_iota(jnp.int32, (256, 512), 0) + core * 256
            kpos = lax.broadcasted_iota(jnp.int32, (256, 512), 1)
            diag = jnp.where(kpos <= qpos, s[:, n - 512:], -jnp.inf)
            s = diag if b == 0 else jnp.concatenate([s[:, :n - 512], diag], axis=1)
            top = jnp.max(s, axis=1, keepdims=True)
            e = jnp.exp2((s - top) * scale)
            inv = 1.0 / jnp.sum(e, axis=1, keepdims=True)
            ctx = (jnp.dot(e.astype(BF), values, preferred_element_type=F32) * inv).astype(BF)
            ctx = ctx.reshape(4, 2, 32, HD)
            for m in range(4):
                C[0, b, core, a_own, m] = ctx[m, 0]
                C[1, m, core, a_own, b] = ctx[m, 1]

    dctx, cs = {}, {}

    def send_ctx(t):
        hf, k = ORDER_OUT[t]
        ref = C.at[hf, (lead[hf] + k) % 4, core, a_own]
        dctx[t] = [copy(ref, ref, to) for to in (hup, hdn, hop)]
        pending.extend([(d, p > 0) for d in dctx[t]])

        @pl.when(p > 0)
        def _():
            for d in dctx[t]:
                d.start()

    def stage_b(t):
        hf, k = ORDER_OUT[t]
        for d, cond in zip(dctx[t], (p != 1, p != 3, p != 2)):
            pl.when(cond)(d.wait_recv)
        ref = C.at[hf, (lead[hf] + k) % 4, core]
        cs[t] = go(copy(ref, ref, sib))

    e1, u1 = {}, {}

    def stage_c(t):
        hf, k = ORDER_OUT[t]
        l = (lead[hf] + k) % 4
        cs[t].wait_recv()

        def project(g):
            rows = jnp.concatenate([C[hf, l, g, a].reshape(128, HD) for a in range(3)], axis=1)
            return jnp.dot(rows, WO[...], preferred_element_type=F32).reshape(4, 32, FEAT)

        for g in ((1, 0) if k == 1 else (0, 1)):
            if k == 0:
                T[hf, g] = project(g)
                continue
            PO[t, g] = project(g).astype(BF)
            if k == 2:
                e1[hf, g] = go(copy(PO.at[t, g], H1.at[hf, g], at_lead[hf](1 + 2 * g)))
            elif (k, g) in ((1, 1), (3, 0)):
                u1[hf, 1 - g, g] = go(copy(PO.at[t, g], U1.at[hf, 1 - g, g], at_lead[hf](k)))

    def stage_d(hf, g):
        k = 1 if g == 0 else 3
        t = ORDER_OUT.index((hf, k))
        e1[hf, g].wait_recv()
        for step in (2, 1, 3, 0):
            mi = (minor[hf] + step) % 4
            PO[t, g, mi] = (PO[t, g, mi].astype(F32) + H1[hf, g, mi].astype(F32)).astype(BF)
            u1[hf, g, g, step] = go(copy(PO.at[t, g, mi], U1.at[hf, g, g, mi], at_lead[hf](k)))

    stages = dict(S=send_ctx, B=stage_b, C=stage_c, D=lambda i: stage_d(i // 2, i % 2))
    for word in SCHEDULE_OUT:
        stages[word[0]](int(word[1:]))

    e2, u2, ez = {}, {}, {}

    def add(hf, g, step):
        mi = (minor[hf] + step) % 4
        u1[hf, g, g, step].wait_recv()
        t_ = T[hf, g, mi] + U1[hf, 0, g, mi].astype(F32) + U1[hf, 1, g, mi].astype(F32)
        T[hf, g, mi] = t_
        return t_.astype(BF)

    for hf in range(2):
        to = at_minor[hf]
        u1[hf, 0, 1].wait_recv()
        u1[hf, 1, 0].wait_recv()
        for g in range(2):
            ZS[hf, 0, g] = add(hf, g, 2)
            e2[hf, g] = go(copy(ZS.at[hf, 0, g], H2.at[hf, g], to(1 + 2 * g)))
    for hf in range(2):
        to = at_minor[hf]
        ZS[hf, 1, 1] = add(hf, 1, 1)
        u2[hf, 0, 1] = go(copy(ZS.at[hf, 1, 1], U2.at[hf, 0, 1], to(1)))
        ZS[hf, 2, 0] = add(hf, 0, 3)
        u2[hf, 1, 0] = go(copy(ZS.at[hf, 2, 0], U2.at[hf, 1, 0], to(3)))
    for hf in range(2):
        for g, step in ((0, 1), (1, 3), (0, 0), (1, 0)):
            add(hf, g, step)
    for hf in range(2):
        m, to = minor[hf], at_minor[hf]
        mp, mm = (m + 1) % 4, (m + 3) % 4
        e2[hf, 0].wait_recv()
        ZS[hf, 1, 0] = (T[hf, 0, mp] + H2[hf, 0].astype(F32)).astype(BF)
        u2[hf, 0, 0] = go(copy(ZS.at[hf, 1, 0], U2.at[hf, 0, 0], to(1)))
        e2[hf, 1].wait_recv()
        ZS[hf, 2, 1] = (T[hf, 1, mm] + H2[hf, 1].astype(F32)).astype(BF)
        u2[hf, 1, 1] = go(copy(ZS.at[hf, 2, 1], U2.at[hf, 1, 1], to(3)))
    for hf in range(2):
        m = minor[hf]
        for dr in range(2):
            for g in range(2):
                u2[hf, dr, g].wait_recv()
        g = 1 - zl
        ZS[hf, 3, 0] = (T[hf, g, m] + U2[hf, 0, g].astype(F32) + U2[hf, 1, g].astype(F32)).astype(BF)
        ez[hf] = go(copy(ZS.at[hf, 3, 0], Z.at[hf], zpart))
    for hf in range(2):
        m = minor[hf]
        rows = slice(hf * 32, hf * 32 + 32)
        own = T[hf, zl, m] + U2[hf, 0, zl].astype(F32) + U2[hf, 1, zl].astype(F32)
        own = own + tok[rows].astype(F32) + bout[...].reshape(1, FEAT)
        ez[hf].wait_recv()
        out[rows] = (own + Z[hf].astype(F32)).astype(BF)

    for d, cond in pending:
        if cond is None:
            d.wait_send()
        else:
            pl.when(cond)(d.wait_send)


SCRATCH = [
    pltpu.VMEM((3, FEAT, UNIT), BF),
    pltpu.VMEM((UNIT, FEAT), BF),
    pltpu.VMEM((64, FEAT), BF),
    pltpu.VMEM((2, 4, 2, 4, 32, FEAT), BF),
    pltpu.VMEM((FEAT, 3 * UNIT), BF),
    pltpu.VMEM((UNIT, FEAT), BF),
    pltpu.VMEM((3, 8, UNIT), F32),
    pltpu.VMEM((10, 8, 128), F32),
    pltpu.VMEM((3, 1024, UNIT), F32),
    pltpu.VMEM((3, 1024, UNIT), BF),
    pltpu.VMEM((3, 1024, UNIT), BF),
    pltpu.VMEM((1024, UNIT), BF),
    pltpu.VMEM((1024, UNIT), BF),
    pltpu.VMEM((2, 1024, UNIT), BF),
    pltpu.VMEM((2, 512, UNIT), BF),
    pltpu.VMEM((2, 512, UNIT), BF),
    pltpu.VMEM((4, 4, 2, 32, HD), BF),
    pltpu.VMEM((2, 4, 2, 4, 2, 32, HD), BF),
    pltpu.VMEM((2, 4, 2, 3, 4, 32, HD), BF),
    pltpu.VMEM((6, 2, 4, 32, FEAT), BF),
    pltpu.VMEM((2, 2, 4, 32, FEAT), BF),
    pltpu.VMEM((2, 2, 2, 4, 32, FEAT), BF),
    pltpu.VMEM((2, 2, 4, 32, FEAT), F32),
    pltpu.VMEM((2, 2, 32, FEAT), BF),
    pltpu.VMEM((2, 2, 2, 32, FEAT), BF),
    pltpu.VMEM((2, 32, FEAT), BF),
    pltpu.VMEM((2, 4, 2, 32, FEAT), BF),
    pltpu.SemaphoreType.DMA((256,)),
    pltpu.SemaphoreType.DMA((256,)),
    pltpu.SemaphoreType.DMA((2,)),
]


def body(tokens, ln_gain, ln_bias, w_qkv, bias_qkv, mask_qkv, w_out, bias_out, mask_out):
    vm = pl.BlockSpec(memory_space=pltpu.VMEM)
    hbm = pl.BlockSpec(memory_space=pl.ANY)
    sm = pl.BlockSpec(memory_space=pltpu.SMEM)
    return pl.pallas_call(
        kernel,
        out_shape=jax.ShapeDtypeStruct((64, FEAT), BF),
        in_specs=[vm, vm, vm, hbm, vm, sm, hbm, vm, sm],
        out_specs=vm,
        scratch_shapes=SCRATCH,
        compiler_params=pltpu.CompilerParams(
            collective_id=0, has_side_effects=True, vmem_limit_bytes=60 * 1024 * 1024),
    )(tokens, ln_gain, ln_bias, w_qkv, bias_qkv, jnp.swapaxes(mask_qkv, 1, 2), w_out, bias_out, mask_out)


def solution(mesh):
    placed = (
        P("col", "row"),
        P("row"),
        P("row"),
        P(None, "row", "col"),
        P(None, "col"),
        P(None, "row", "col"),
        P("col", "row"),
        P("row"),
        P("col", "row"),
    )
    return jax.shard_map(
        body, mesh=mesh, in_specs=placed, out_specs=P("col", "row"), check_vma=False
    )
```
